256 devices in a mesh: xy: 32 (over z, x_lo, core), gz: 8 (over x_hi, y).
Axes of the slice: x: 4 (x_hi: 2, x_lo: 2; x = x_hi * 2 + x_lo), y: 4, z: 8, core: 2. Of those that a mesh axis runs over, the one named last changes fastest.
Arguments:
- features: float32 [524288, 128], P(('xy', 'gz')), may hold values from -6 to 6
- positions: float32 [2, 524288], P(None, ('xy', 'gz')), may hold values from 0 to 1
- plane_index: int32 [524288], P(('xy', 'gz')), may hold values from 0 to 2
- plane_frac: float32 [524288], P(('xy', 'gz')), may hold values from 0 to 1
- neighbours: int32 [16, 524288], P(None, ('xy', 'gz')), may hold values from 0 to 3071
- pair_weight: float32 [16, 524288], P(None, ('xy', 'gz')), may hold values from 0.05 to 0.5
- ghost_index: int32 [65536], P(('xy', 'gz')), may hold values from 0 to 2047
- wave_index: int32 [2, 512], replicated, may hold values from -12 to 12, as said below
- channel_filter: float32 [512, 128], replicated, may hold values from -6 to 6
- screening: float32 [32], P('gz'), may hold values from 4 to 96
- w_short: float32 [128, 128], replicated, may hold values from -0.5 to 0.5
Outputs:
- messages: float32 [524288, 128], P(('xy', 'gz'))
The draws below stay inside these ranges and needn't reach their ends.
Inputs may be any that keep to these rules, and one draw needn't show every extreme that they name: `wave_index`: the wavevector pairs are distinct.
All inputs are finite; a program needn't handle non-finite values.
Results may differ from the reference program's by a relative error of at most 0.0015.
Values may be sent and summed in bfloat16 or wider, within the bound.
No kernel may reach another device: no remote copies, remote signals or barrier semaphores. Data moves between devices by JAX's collectives and lax.ppermute only.
A program may use at most 64 MiB of HBM per device.

```python
import math
import jax
import jax.numpy as jnp
from jax import lax

C = 128
K = 512
ATOM_DEV = 2048
NBR = 16
PLANES = 4
GHOST = 256
ATOMS = 524288
NZ = 32
GHOST_ALL = 65536
N_XY = 32
N_GZ = 8


def draw_wave_index(key, part):
    chosen = jax.random.permutation(key, 625)[:K]
    wave_x = chosen // 25 - 12
    wave_y = chosen % 25 - 12
    return jnp.stack([wave_x, wave_y]).astype(jnp.int32)


def plant(drawn, key, low, high):
    longest = drawn.shape.index(max(drawn.shape))
    spots = []
    for shift in (0, 1):
        where = [jax.random.randint(jax.random.fold_in(key, axis), (), 0, length) for axis, length in enumerate(drawn.shape)]
        where[longest] = (where[longest] + shift) % drawn.shape[longest]
        spots.append(tuple(where))
    return drawn.at[spots[0]].set(low).at[spots[1]].set(high)


def levels(stream_key, shape, pieces, least, high):
    def one(position, shards_of):
        heights = jax.random.uniform(jax.random.fold_in(jax.random.fold_in(stream_key, 6), position), (shards_of,), jnp.float32, least / len(pieces), high / len(pieces))
        return jnp.repeat(jnp.exp(heights), shape[position] // shards_of).reshape((-1,) + (1,) * (len(shape) - position - 1))

    level = one(*pieces[0])
    for cut in pieces[1:]:
        level = level * one(*cut)
    return level


def bell_draw(stream_key, shape, width, most, cuts=(), kind=jnp.bfloat16):
    gain = levels(stream_key, shape, cuts, -0.22, 0.18) if cuts else 1.0
    drawn = jax.random.normal(stream_key, shape, jnp.float32) * width * gain
    return jnp.minimum(jnp.maximum(drawn, -most), most).astype(kind)


def setup_inputs(seed: int = 0) -> dict:
    splits = jax.random.split(jax.random.key(seed), 12)
    features = bell_draw(splits[0], (ATOMS, C), 1.0, 6.0, ((0, 256),), jnp.float32)
    positions = jnp.clip(1.0 * jax.random.uniform(splits[1], (2, ATOMS), jnp.float32) ** levels(splits[1], (2, ATOMS), ((1, 256),), -0.2, 0.2), 0.0, 1.0)
    plane_index = plant(jax.random.randint(splits[2], (ATOMS,), 0, PLANES - 1), jax.random.fold_in(splits[2], 1), 0, (PLANES - 1) - 1).astype(jnp.int32)
    plane_frac = jnp.clip(1.0 * jax.random.uniform(splits[3], (ATOMS,), jnp.float32) ** levels(splits[3], (ATOMS,), ((0, 256),), -0.2, 0.2), 0.0, 1.0)
    neighbours = plant(jax.random.randint(splits[4], (NBR, ATOMS), 0, ATOM_DEV + 4 * GHOST), jax.random.fold_in(splits[4], 1), 0, (ATOM_DEV + 4 * GHOST) - 1).astype(jnp.int32)
    pair_weight = jnp.clip(0.05 + 0.45 * jax.random.uniform(splits[5], (NBR, ATOMS), jnp.float32) ** levels(splits[5], (NBR, ATOMS), ((1, 256),), -0.2, 0.2), 0.05, 0.5)
    ghost_index = plant(jax.random.randint(splits[6], (GHOST_ALL,), 0, ATOM_DEV), jax.random.fold_in(splits[6], 1), 0, ATOM_DEV - 1).astype(jnp.int32)
    wave_index = draw_wave_index(jax.random.fold_in(splits[11], 71), 0)
    channel_filter = bell_draw(splits[8], (K, C), 1.0, 6.0, (), jnp.float32)
    screening = jnp.clip(jnp.exp(math.log(96.0) - 3.1780538 * jax.random.uniform(splits[9], (NZ,), jnp.float32) ** levels(splits[9], (NZ,), ((0, 8),), -0.2, 0.2)), 4.0, 96.0)
    w_short = bell_draw(splits[10], (C, C), C ** -0.5, 0.5, (), jnp.float32)
    return dict(features=features, positions=positions, plane_index=plane_index, plane_frac=plane_frac, neighbours=neighbours, pair_weight=pair_weight, ghost_index=ghost_index, wave_index=wave_index, channel_filter=channel_filter, screening=screening, w_short=w_short)


two_pi = 2.0 * math.pi
plane_gap = 0.01
long_gain = 0.125

def kernels(wave_index, screening):
    wave_x = wave_index[0].astype(jnp.float32)
    wave_y = wave_index[1].astype(jnp.float32)
    radial = two_pi * two_pi * (wave_x * wave_x + wave_y * wave_y)
    spatial = jnp.sqrt(radial[None, :] + (screening * screening)[:, None])
    return (jnp.exp(-plane_gap * spatial), two_pi / spatial)

def phase_rows(pos_x, pos_y, wave_index):
    wave_x = wave_index[0].astype(jnp.float32)
    wave_y = wave_index[1].astype(jnp.float32)
    phase_angle = two_pi * (pos_x[:, None] * wave_x[None, :] + pos_y[:, None] * wave_y[None, :])
    stacked = jnp.stack([jnp.cos(phase_angle), -jnp.sin(phase_angle)], axis=-1)
    return stacked.reshape(pos_x.shape[0], -1).astype(jnp.bfloat16)

def hat_rows(plane_index, plane_frac, plane_count):
    slot_ids = jnp.arange(plane_count, dtype=jnp.int32)[None, :]
    low_plane = plane_index[:, None]
    frac_col = plane_frac[:, None]
    return jnp.where(slot_ids == low_plane, 1.0 - frac_col, 0.0) + jnp.where(slot_ids == low_plane + 1, frac_col, 0.0)

def reference(features, positions, plane_index, plane_frac, neighbours, pair_weight, ghost_index, wave_index, channel_filter, screening, w_short):
    devices = N_XY * N_GZ
    feat_grid = features.reshape(N_XY, N_GZ, ATOM_DEV, C)
    ghosts = ghost_index.reshape(N_XY, N_GZ, GHOST)
    sent_rows = jax.vmap(jax.vmap(lambda source_rows, index_rows: source_rows[index_rows]))(feat_grid, ghosts)
    empty_rows = jnp.zeros_like(sent_rows[:, :1])
    from_below = jnp.concatenate([empty_rows, sent_rows[:, :-1]], axis=1)
    from_above = jnp.concatenate([sent_rows[:, 1:], empty_rows], axis=1)
    lookup_table = jnp.concatenate([feat_grid, jnp.roll(sent_rows, 1, axis=0), jnp.roll(sent_rows, -1, axis=0), from_below, from_above], axis=2)
    lookup_table = lookup_table.reshape(devices, ATOM_DEV + 4 * GHOST, C)
    near_index = neighbours.reshape(NBR, devices, ATOM_DEV).transpose(1, 0, 2)
    near_weight = pair_weight.reshape(NBR, devices, ATOM_DEV).transpose(1, 0, 2)

    def short_one(pair_item):
        table_one, index_one, weight_one = pair_item
        pair_sum = lax.optimization_barrier(jnp.sum(weight_one[:, :, None] * table_one[index_one], axis=0))
        return jnp.dot(pair_sum, w_short, precision=lax.Precision.HIGHEST)
    short_range = lax.map(short_one, (lookup_table, near_index, near_weight))
    pos_grid = positions.reshape(2, devices, ATOM_DEV)
    low_grid = plane_index.reshape(devices, ATOM_DEV)
    frac_grid = plane_frac.reshape(devices, ATOM_DEV)
    feat_flat = features.reshape(devices, ATOM_DEV, C)
    norm_scale = float(ATOM_DEV * N_XY) ** (-0.5)

    def structure_one(pair_item):
        pos_x, pos_y, low_plane, frac_one, feat_one = pair_item
        phase_table = phase_rows(pos_x, pos_y, wave_index)
        hat_table = hat_rows(low_plane, frac_one, PLANES)
        weighted = (hat_table[:, :, None] * feat_one[:, None, :]).reshape(ATOM_DEV, PLANES * C).astype(jnp.bfloat16)
        return jnp.dot(phase_table.astype(jnp.float32).T, weighted.astype(jnp.float32), precision=lax.Precision.HIGHEST) * norm_scale
    terms = lax.map(structure_one, (pos_grid[0], pos_grid[1], low_grid, frac_grid, feat_flat))
    structure = lax.optimization_barrier(jnp.sum(terms.reshape(N_XY, N_GZ, 2 * K, PLANES * C), axis=0))
    source = structure.reshape(N_GZ, K, 2, PLANES, C).transpose(0, 3, 1, 2, 4).reshape(NZ, K, 2, C)
    decay_rate, kernel = kernels(wave_index, screening)

    def step_chain(state, chain_item):
        rate_row, source_row = chain_item
        state = rate_row[:, None, None] * state + source_row
        return (state, state)
    start_state = jnp.zeros((K, 2, C), jnp.float32)
    forward = lax.scan(step_chain, start_state, (decay_rate, source))[1]
    backward = lax.scan(step_chain, start_state, (decay_rate, source), reverse=True)[1]
    potential = long_gain * kernel[:, :, None, None] * channel_filter[None, :, None, :] * (forward + backward - source)
    potential = potential.astype(jnp.bfloat16)
    field_layers = potential.reshape(N_GZ, PLANES, K, 2, C).transpose(0, 2, 3, 1, 4).reshape(N_GZ, 2 * K, PLANES * C)
    layer_ids = (jnp.arange(devices, dtype=jnp.int32) % N_GZ).astype(jnp.int32)

    def long_one(pair_item):
        pos_x, pos_y, low_plane, frac_one, layer_at = pair_item
        phase_table = phase_rows(pos_x, pos_y, wave_index)
        hat_table = hat_rows(low_plane, frac_one, PLANES)
        layer_field = field_layers[layer_at]
        projected = jnp.dot(phase_table.astype(jnp.float32), layer_field.astype(jnp.float32), precision=lax.Precision.HIGHEST)
        return lax.optimization_barrier(jnp.sum(hat_table[:, :, None] * projected.reshape(ATOM_DEV, PLANES, C), axis=1))
    long_range = lax.map(long_one, (pos_grid[0], pos_grid[1], low_grid, frac_grid, layer_ids))
    return (short_range + long_range).reshape(ATOMS, C)
```

```python
import math

import jax
import jax.numpy as jnp
from jax import lax
from jax.experimental import pallas as pl
from jax.experimental.pallas import tpu as pltpu
from jax.sharding import Mesh
from jax.sharding import PartitionSpec as P

two_pi = 2.0 * math.pi
plane_gap = 0.01
long_gain = 0.125

ATOMS = 2048
CHAN = 128
PLANES = 4
COLS = PLANES * CHAN
NBR = 16
GHOST = 256
TABLE = ATOMS + 4 * GHOST
LAYERS = 8
XY_DEVICES = 32
CHUNK = 24
CHUNKS = 16
HALF = CHUNKS * CHUNK
USED = 14 * CHUNK
PAYLOAD = 32

SPLIT = ("z", "xl", "core", "xh", "y")
LATERAL = ("z", "xl", "core")
SWAP = ("z", "xl")
VERTICAL = ("xh", "y")

smem = pl.BlockSpec(memory_space=pltpu.SMEM)
vmem = pl.BlockSpec(memory_space=pltpu.VMEM)


def cost(flops, nbytes):
    return pl.CostEstimate(flops=flops, bytes_accessed=nbytes, transcendentals=0)


def params(mebibytes=40):
    return pltpu.CompilerParams(vmem_limit_bytes=mebibytes << 20)


BLOCK = 512


def structure_kernel(meta, pos, low, frac, feat, phase, hat, own, other, weighted):
    tile_row = lax.broadcasted_iota(jnp.int32, (8, BLOCK), 0)
    upper = tile_row >= 4
    role = tile_row & 3
    wave_is_sin_x = (role == 1) | (role == 2)
    wave_is_sin_y = (role & 1) == 1
    orders = lax.broadcasted_iota(jnp.int32, (16, BLOCK), 0).astype(jnp.float32)

    def row(table, at):
        return jnp.broadcast_to(table[at : at + 1, :], (8, BLOCK))

    def block(at, _):
        lanes = pl.ds(pl.multiple_of(at * BLOCK, BLOCK), BLOCK)

        def tables(coordinate):
            turns = orders * coordinate
            turns = turns - jnp.floor(turns + 0.5)
            angle = two_pi * turns
            return jnp.cos(angle), jnp.sin(angle)

        cos_x, sin_x = tables(pos[0:1, lanes])
        cos_y, sin_y = tables(pos[1:2, lanes])
        for half in range(2):
            b_tiles, axis_tiles = [], []
            for tile in range(3):
                n = 6 * half + 1 + 2 * tile
                cos_n = jnp.where(upper, row(cos_y, n + 1), row(cos_y, n))
                sin_n = jnp.where(upper, row(sin_y, n + 1), row(sin_y, n))
                b_tiles.append(jnp.where(wave_is_sin_y, sin_n, cos_n))
                cos_m = jnp.where(upper, row(cos_x, n + 1), row(cos_x, n))
                sin_m = jnp.where(upper, row(sin_x, n + 1), row(sin_x, n))
                axis_tiles.append(
                    jnp.where(
                        role == 0,
                        cos_n,
                        jnp.where(role == 1, cos_m, jnp.where(role == 2, sin_m, sin_n)),
                    )
                )
            for pair in range(6):
                parts = []
                for a in (2 * pair + 1, 2 * pair + 2):
                    a_tile = jnp.where(wave_is_sin_x, row(sin_x, a), row(cos_x, a))
                    parts += [a_tile * b_tile for b_tile in b_tiles]
                rows = half * USED + pair * 2 * CHUNK
                phase[rows : rows + 2 * CHUNK, lanes] = jnp.concatenate(parts, axis=0).astype(
                    jnp.bfloat16
                )
            zero = jnp.zeros((8, BLOCK), jnp.float32)
            first = jnp.where(tile_row == 0, 1.0, 0.0) if half == 0 else zero
            rows = half * USED + 12 * CHUNK
            phase[rows : rows + 2 * CHUNK, lanes] = jnp.concatenate(
                axis_tiles + [first, zero, zero], axis=0
            ).astype(jnp.bfloat16)

        low_plane = low[:, lanes]
        height = frac[:, lanes]
        hat_block = jnp.where(tile_row == low_plane, 1.0 - height, 0.0) + jnp.where(
            tile_row == low_plane + 1, height, 0.0
        )
        hat[:, lanes] = hat_block
        hat_cols = jnp.transpose(hat_block)
        feat_block = feat[lanes, :]
        for plane in range(PLANES):
            weighted[lanes, plane * CHAN : (plane + 1) * CHAN] = (
                hat_cols[:, plane : plane + 1] * feat_block
            ).astype(jnp.bfloat16)
        return 0

    lax.fori_loop(0, ATOMS // BLOCK, block, 0)
    core = meta[0]
    for mine in (False, True):
        start = pl.multiple_of((core if mine else 1 - core) * USED, 16)
        sums = jnp.dot(
            phase[pl.ds(start, USED), :], weighted[...], preferred_element_type=jnp.float32
        )
        rest = jnp.zeros((HALF - USED, COLS), jnp.float32)
        if mine:
            own[0:USED, :] = sums
            own[USED:HALF, :] = rest
        else:
            other[0:USED, :] = sums.astype(jnp.bfloat16)
            other[USED:HALF, :] = rest.astype(jnp.bfloat16)


def local_structure(meta, positions, low, frac, features):
    return pl.pallas_call(
        structure_kernel,
        out_shape=(
            jax.ShapeDtypeStruct((2 * USED, ATOMS), jnp.bfloat16),
            jax.ShapeDtypeStruct((8, ATOMS), jnp.float32),
            jax.ShapeDtypeStruct((HALF, COLS), jnp.float32),
            jax.ShapeDtypeStruct((HALF, COLS), jnp.bfloat16),
        ),
        in_specs=[smem, vmem, vmem, vmem, vmem],
        out_specs=(vmem, vmem, vmem, vmem),
        scratch_shapes=[pltpu.VMEM((ATOMS, COLS), jnp.bfloat16)],
        cost_estimate=cost(1_500_000_000, 8_000_000),
        compiler_params=params(),
        name="local_structure",
    )(meta, positions, low, frac, features)


def wave_square(half, chunk):
    place = lax.broadcasted_iota(jnp.int32, (CHUNK, CHAN), 0)
    n = 6 * half + 1 + (place >> 2)
    n_square = jnp.where(chunk <= 12, n * n, 0)
    a_square = jnp.where(chunk < 12, (chunk + 1) * (chunk + 1), 0)
    return (n_square + a_square).astype(jnp.float32)


def coefficient_kernel(meta, waves, filters, alpha, beta):
    half, chunk = meta[0], meta[1]
    place = lax.broadcasted_iota(jnp.int32, (CHUNK, 512), 0)
    role = place & 3
    n = 6 * half + 1 + (place >> 2)
    along_x = (role == 1) | (role == 2)
    only_zero = jnp.where((place == 0) & (chunk == 13) & (half == 0), 0, -1)
    a = jnp.where(chunk < 12, chunk + 1, jnp.where(chunk == 12, jnp.where(along_x, n, 0), only_zero))
    b = jnp.where(chunk < 12, n, jnp.where(chunk == 12, jnp.where(along_x, 0, n), only_zero))
    kx, ky = waves[0:1, :], waves[1:2, :]
    hit = jnp.where((jnp.abs(kx) == a) & (jnp.abs(ky) == b), 1.0, 0.0)
    product = kx * ky
    sign = jnp.where(product > 0, 1.0, jnp.where(product < 0, -1.0, 0.0))
    signed = hit * sign * jnp.where(role < 2, -1.0, 1.0)
    both = jnp.dot(
        jnp.concatenate([hit, signed], axis=0),
        filters[...],
        preferred_element_type=jnp.float32,
        precision=lax.Precision.HIGHEST,
    )
    alpha[...] = both[0:CHUNK]
    beta[...] = both[CHUNK : 2 * CHUNK]


def coefficients(meta, waves, filters):
    return pl.pallas_call(
        coefficient_kernel,
        out_shape=(jax.ShapeDtypeStruct((CHUNK, CHAN), jnp.float32),) * 2,
        in_specs=[smem, vmem, vmem],
        out_specs=(vmem, vmem),
        cost_estimate=cost(40_000_000, 300_000),
        compiler_params=params(),
        name="coefficients",
    )(meta, waves, filters)


def spatial_wave(square, screen):
    return jnp.sqrt((two_pi * two_pi) * square + screen * screen)


def source_kernel(meta, screening, parts, source, payload):
    total = parts[0].astype(jnp.float32)
    for at in range(1, CHUNKS):
        total = total + parts[at].astype(jnp.float32)
    total = total * float(ATOMS * XY_DEVICES) ** -0.5
    source[...] = total
    square = wave_square(meta[0], meta[1])
    decay = [
        jnp.exp(-plane_gap * spatial_wave(square, screening[plane])) for plane in range(PLANES)
    ]
    planes = [total[:, plane * CHAN : (plane + 1) * CHAN] for plane in range(PLANES)]
    upward = planes[0]
    for plane in range(1, PLANES):
        upward = decay[plane] * upward + planes[plane]
    downward = planes[PLANES - 1]
    for plane in reversed(range(PLANES - 1)):
        downward = decay[plane] * downward + planes[plane]
    layer = meta[2]
    which = lax.broadcasted_iota(jnp.int32, (8, CHAN), 0)
    screens = jnp.zeros((8, CHAN), jnp.float32)
    for plane in range(PLANES):
        screens = jnp.where(which == plane, screening[plane], screens)
    for target in range(LAYERS):
        payload[target, 0:CHUNK, :] = jnp.where(layer < target, upward, downward)
        payload[target, CHUNK:PAYLOAD, :] = screens


def local_source(meta, screening, parts):
    return pl.pallas_call(
        source_kernel,
        out_shape=(
            jax.ShapeDtypeStruct((CHUNK, COLS), jnp.float32),
            jax.ShapeDtypeStruct((LAYERS, PAYLOAD, CHAN), jnp.float32),
        ),
        in_specs=[smem, smem, vmem],
        out_specs=(vmem, vmem),
        cost_estimate=cost(1_000_000, 600_000),
        compiler_params=params(),
        name="local_source",
    )(meta, screening, parts)


def potential_kernel(meta, screening, source, carried, alpha, beta, out):
    square = wave_square(meta[0], meta[1])
    layer = meta[2]
    upward = jnp.zeros((CHUNK, CHAN), jnp.float32)
    downward = jnp.zeros((CHUNK, CHAN), jnp.float32)
    scales = []
    for at in range(LAYERS):
        depth = jnp.zeros((CHUNK, CHAN), jnp.float32)
        for plane in range(PLANES):
            depth = depth + spatial_wave(square, carried[at, CHUNK + plane : CHUNK + plane + 1, :])
        scales.append(jnp.exp(-plane_gap * depth))
    for at in range(LAYERS):
        upward = jnp.where(at < layer, scales[at] * upward + carried[at, 0:CHUNK, :], upward)
    for at in reversed(range(LAYERS)):
        downward = jnp.where(at > layer, scales[at] * downward + carried[at, 0:CHUNK, :], downward)
    spatial = [spatial_wave(square, screening[plane]) for plane in range(PLANES)]
    decay = [jnp.exp(-plane_gap * s) for s in spatial]
    planes = [source[:, plane * CHAN : (plane + 1) * CHAN] for plane in range(PLANES)]
    sums = []
    for plane in range(PLANES):
        upward = decay[plane] * upward + planes[plane]
        sums.append(upward - planes[plane])
    for plane in reversed(range(PLANES)):
        downward = decay[plane] * downward + planes[plane]
        sums[plane] = sums[plane] + downward
    odd = (lax.broadcasted_iota(jnp.int32, (CHUNK, CHAN), 0) & 1) == 1
    results = []
    for plane in range(PLANES):
        field = sums[plane]
        partner = jnp.where(odd, pltpu.roll(field, 1, 0), pltpu.roll(field, CHUNK - 1, 0))
        mixed = alpha[...] * field + beta[...] * partner
        results.append((long_gain * two_pi) / spatial[plane] * mixed)
    full = jnp.concatenate(results, axis=1).astype(jnp.bfloat16)
    for at in range(CHUNKS):
        out[at] = full


def local_potential(meta, screening, source, carried, alpha, beta):
    return pl.pallas_call(
        potential_kernel,
        out_shape=jax.ShapeDtypeStruct((CHUNKS, CHUNK, COLS), jnp.bfloat16),
        in_specs=[smem, smem, vmem, vmem, vmem, vmem],
        out_specs=vmem,
        cost_estimate=cost(1_000_000, 1_000_000),
        compiler_params=params(),
        name="local_potential",
    )(meta, screening, source, carried, alpha, beta)


def ghost_kernel(rows, feat, out):
    def eight(at, _):
        for k in range(8):
            out[at * 8 + k] = feat[rows[at * 8 + k]]
        return 0

    lax.fori_loop(0, GHOST // 8, eight, 0)


def ghost_rows(rows, feat):
    return pl.pallas_call(
        ghost_kernel,
        out_shape=jax.ShapeDtypeStruct((GHOST, 1, CHAN), jnp.float32),
        in_specs=[smem, vmem],
        out_specs=vmem,
        cost_estimate=cost(1_000, 1_000_000),
        compiler_params=params(),
        name="ghost_rows",
    )(rows, feat)


def pair_messages(index, weight, table, w_short, name):
    count = weight.shape[0]

    def kernel(slots, weights, rows, projection, out, sums):
        place = lax.broadcasted_iota(jnp.int32, (8, CHAN), 0)

        def eight(at, _):
            base = pl.multiple_of(at * 8, 8)
            factor = weights[pl.ds(base, 8), :]
            total = jnp.zeros((8, CHAN), jnp.float32)
            for k in range(NBR):
                picked = jnp.broadcast_to(rows[slots[k * count + base]], (8, CHAN))
                for s in range(1, 8):
                    found = jnp.broadcast_to(rows[slots[k * count + base + s]], (8, CHAN))
                    picked = jnp.where(place == s, found, picked)
                total = total + picked * factor[:, k : k + 1]
            sums[pl.ds(base, 8), :] = total
            return 0

        lax.fori_loop(0, count // 8, eight, 0)
        out[...] = jnp.dot(
            sums[...],
            projection[...],
            preferred_element_type=jnp.float32,
            precision=lax.Precision.HIGHEST,
        )

    return pl.pallas_call(
        kernel,
        out_shape=jax.ShapeDtypeStruct((count, CHAN), jnp.float32),
        in_specs=[smem, vmem, vmem, vmem],
        out_specs=vmem,
        scratch_shapes=[pltpu.VMEM((count, CHAN), jnp.float32)],
        cost_estimate=cost(count * 200_000, count * 57_000),
        compiler_params=params(),
        name=name,
    )(index.reshape(-1), weight, table, w_short)


def project_kernel(meta, mine, theirs, phase, hat, short, out):
    core = meta[0]
    dims = (((0,), (0,)), ((), ()))
    near = pl.multiple_of(core * USED, 16)
    far = pl.multiple_of((1 - core) * USED, 16)
    projected = lax.dot_general(
        mine[0:USED, :], phase[pl.ds(near, USED), :], dims, preferred_element_type=jnp.float32
    ) + lax.dot_general(
        theirs[0:USED, :], phase[pl.ds(far, USED), :], dims, preferred_element_type=jnp.float32
    )
    total = hat[0:1, :] * projected[0:CHAN]
    for plane in range(1, PLANES):
        total = total + hat[plane : plane + 1, :] * projected[plane * CHAN : (plane + 1) * CHAN]
    out[...] = jnp.transpose(total) + short[...]


def project(meta, mine, theirs, phase, hat, short):
    return pl.pallas_call(
        project_kernel,
        grid=(ATOMS // BLOCK,),
        out_shape=jax.ShapeDtypeStruct((ATOMS, CHAN), jnp.float32),
        in_specs=[
            smem,
            pl.BlockSpec((HALF, COLS), lambda i: (0, 0)),
            pl.BlockSpec((HALF, COLS), lambda i: (0, 0)),
            pl.BlockSpec((2 * USED, BLOCK), lambda i: (0, i)),
            pl.BlockSpec((8, BLOCK), lambda i: (0, i)),
            pl.BlockSpec((BLOCK, CHAN), lambda i: (i, 0)),
        ],
        out_specs=pl.BlockSpec((BLOCK, CHAN), lambda i: (i, 0)),
        cost_estimate=cost(1_500_000_000, 6_000_000),
        compiler_params=params(),
        name="project",
    )(meta, mine, theirs, phase, hat, short)


PIECES = (512, 640, 896)


def shifted(value, axis, steps):
    count = lax.axis_size(axis)
    return lax.ppermute(value, axis, [(s, (s + steps) % count) for s in range(count)])


def stepped(value, axis, steps):
    devices = range(lax.axis_size(axis))
    return lax.ppermute(value, axis, [(i - steps, i) for i in devices if i - steps in devices])


def other_core(value):
    return lax.ppermute(value, "core", [(0, 1), (1, 0)])


def on_device(
    features,
    positions,
    plane_index,
    plane_frac,
    neighbours,
    pair_weight,
    ghost_index,
    wave_index,
    channel_filter,
    screening,
    w_short,
):
    tie = lax.optimization_barrier
    meta = jnp.stack(
        [lax.axis_index("core"), lax.axis_index(SWAP), lax.axis_index(VERTICAL)]
    ).astype(jnp.int32)
    phase, hat, own, other = local_structure(
        meta, positions, plane_index.reshape(1, -1), plane_frac.reshape(1, -1), features
    )
    joined = (own + other_core(other).astype(jnp.float32)).astype(jnp.bfloat16)
    joined = joined.reshape(CHUNKS, CHUNK, COLS)
    joined, ghost_index, weights = tie((joined, ghost_index, pair_weight))
    parts = lax.all_to_all(joined, SWAP, 0, 0)

    sent = ghost_rows(ghost_index, features.reshape(ATOMS, 1, CHAN)).reshape(GHOST, CHAN)
    sides = [
        shifted(sent, LATERAL, 1),
        shifted(sent, LATERAL, -1),
        stepped(sent, VERTICAL, 1),
        stepped(sent, VERTICAL, -1),
    ]
    table = jnp.concatenate([features] + sides, axis=0).reshape(TABLE, 1, CHAN)
    alpha, beta = coefficients(meta, wave_index, channel_filter)
    weights = weights.T
    first, second = PIECES[0], PIECES[0] + PIECES[1]
    short_a = pair_messages(neighbours[:, :first], weights[:first], table, w_short, "pair_a")

    parts, short_a, alpha, beta = tie((parts, short_a, alpha, beta))
    source, payload = local_source(meta, screening, parts)
    payload, slots_b = tie((payload, neighbours[:, first:second]))
    carried = lax.all_to_all(payload, VERTICAL, 0, 0)
    short_b = pair_messages(slots_b, weights[first:second], table, w_short, "pair_b")

    carried, short_b = tie((carried, short_b))
    field = local_potential(meta, screening, source, carried, alpha, beta)
    field, slots_c = tie((field, neighbours[:, second:]))
    mine = lax.all_to_all(field, SWAP, 0, 0)
    short_c = pair_messages(slots_c, weights[second:], table, w_short, "pair_c")

    mine, short_c = tie((mine, short_c))
    mine = mine.reshape(HALF, COLS)
    theirs = other_core(mine)
    short = jnp.concatenate([short_a, short_b, short_c], axis=0)
    return project(meta, mine, theirs, phase, hat, short)


def solution(mesh):
    split = Mesh(mesh.devices.reshape(8, 2, 2, 2, 4), SPLIT)
    return jax.shard_map(
        on_device,
        mesh=split,
        in_specs=(
            P(SPLIT, None),
            P(None, SPLIT),
            P(SPLIT),
            P(SPLIT),
            P(None, SPLIT),
            P(None, SPLIT),
            P(SPLIT),
            P(),
            P(),
            P(VERTICAL),
            P(),
        ),
        out_specs=P(SPLIT, None),
        check_vma=False,
    )
```

```python
import math

import jax
import jax.numpy as jnp
from jax import lax
from jax.experimental import pallas as pl
from jax.experimental.pallas import tpu as pltpu
from jax.sharding import Mesh
from jax.sharding import PartitionSpec as P

two_pi = 2.0 * math.pi
plane_gap = 0.01
long_gain = 0.125

ATOMS = 2048
CHAN = 128
PLANES = 4
COLS = PLANES * CHAN
NBR = 16
GHOST = 256
TABLE = ATOMS + 4 * GHOST
LAYERS = 8
XY_DEVICES = 32
CHUNK = 24
CHUNKS = 16
HALF = CHUNKS * CHUNK
USED = 14 * CHUNK
PAYLOAD = 32

SPLIT = ("z", "xl", "core", "xh", "y")
LATERAL = ("z", "xl", "core")
SWAP = ("z", "xl")
VERTICAL = ("xh", "y")

smem = pl.BlockSpec(memory_space=pltpu.SMEM)
vmem = pl.BlockSpec(memory_space=pltpu.VMEM)
anywhere = pl.BlockSpec(memory_space=pl.ANY)
hbm = pl.BlockSpec(memory_space=pltpu.HBM)


def cost(flops, nbytes):
    return pl.CostEstimate(flops=flops, bytes_accessed=nbytes, transcendentals=0)


def params(mebibytes=8):
    return pltpu.CompilerParams(vmem_limit_bytes=mebibytes << 20)


BLOCK = 512


def structure_kernel(
    meta,
    positions,
    plane_low,
    plane_height,
    features,
    phase_out,
    hat,
    own,
    other,
    phase,
    weighted,
    pos,
    low,
    frac,
    feat,
    arrived,
    kept,
):
    loads = [
        pltpu.make_async_copy(source, target, arrived.at[at])
        for at, (source, target) in enumerate(
            ((positions, pos), (plane_low, low), (plane_height, frac), (features, feat))
        )
    ]
    for load in loads:
        load.start()
    for load in loads:
        load.wait()
    keep = pltpu.make_async_copy(phase, phase_out, kept)
    tile_row = lax.broadcasted_iota(jnp.int32, (8, BLOCK), 0)
    upper = tile_row >= 4
    role = tile_row & 3
    wave_is_sin_x = (role == 1) | (role == 2)
    wave_is_sin_y = (role & 1) == 1
    orders = lax.broadcasted_iota(jnp.int32, (16, BLOCK), 0).astype(jnp.float32)

    def row(table, at):
        return jnp.broadcast_to(table[at : at + 1, :], (8, BLOCK))

    def block(at, _):
        lanes = pl.ds(pl.multiple_of(at * BLOCK, BLOCK), BLOCK)

        def tables(coordinate):
            turns = orders * coordinate
            turns = turns - jnp.floor(turns + 0.5)
            angle = two_pi * turns
            return jnp.cos(angle), jnp.sin(angle)

        cos_x, sin_x = tables(pos[0:1, lanes])
        cos_y, sin_y = tables(pos[1:2, lanes])
        for half in range(2):
            b_tiles, axis_tiles = [], []
            for tile in range(3):
                n = 6 * half + 1 + 2 * tile
                cos_n = jnp.where(upper, row(cos_y, n + 1), row(cos_y, n))
                sin_n = jnp.where(upper, row(sin_y, n + 1), row(sin_y, n))
                b_tiles.append(jnp.where(wave_is_sin_y, sin_n, cos_n))
                cos_m = jnp.where(upper, row(cos_x, n + 1), row(cos_x, n))
                sin_m = jnp.where(upper, row(sin_x, n + 1), row(sin_x, n))
                axis_tiles.append(
                    jnp.where(
                        role == 0,
                        cos_n,
                        jnp.where(role == 1, cos_m, jnp.where(role == 2, sin_m, sin_n)),
                    )
                )
            for pair in range(6):
                parts = []
                for a in (2 * pair + 1, 2 * pair + 2):
                    a_tile = jnp.where(wave_is_sin_x, row(sin_x, a), row(cos_x, a))
                    parts += [a_tile * b_tile for b_tile in b_tiles]
                rows = half * USED + pair * 2 * CHUNK
                phase[rows : rows + 2 * CHUNK, lanes] = jnp.concatenate(parts, axis=0).astype(
                    jnp.bfloat16
                )
            zero = jnp.zeros((8, BLOCK), jnp.float32)
            first = jnp.where(tile_row == 0, 1.0, 0.0) if half == 0 else zero
            rows = half * USED + 12 * CHUNK
            phase[rows : rows + 2 * CHUNK, lanes] = jnp.concatenate(
                axis_tiles + [first, zero, zero], axis=0
            ).astype(jnp.bfloat16)

        low_plane = low[:, lanes]
        height = frac[:, lanes]
        hat_block = jnp.where(tile_row == low_plane, 1.0 - height, 0.0) + jnp.where(
            tile_row == low_plane + 1, height, 0.0
        )
        hat[:, lanes] = hat_block
        hat_cols = jnp.transpose(hat_block)
        feat_block = feat[lanes, :]
        for plane in range(PLANES):
            weighted[lanes, plane * CHAN : (plane + 1) * CHAN] = (
                hat_cols[:, plane : plane + 1] * feat_block
            ).astype(jnp.bfloat16)
        return 0

    lax.fori_loop(0, ATOMS // BLOCK, block, 0)
    keep.start()
    core = meta[0]
    for mine in (False, True):
        start = pl.multiple_of((core if mine else 1 - core) * USED, 16)
        sums = jnp.dot(
            phase[pl.ds(start, USED), :], weighted[...], preferred_element_type=jnp.float32
        )
        rest = jnp.zeros((HALF - USED, COLS), jnp.float32)
        if mine:
            own[0:USED, :] = sums
            own[USED:HALF, :] = rest
        else:
            other[0:USED, :] = sums.astype(jnp.bfloat16)
            other[USED:HALF, :] = rest.astype(jnp.bfloat16)
    keep.wait()


def local_structure(meta, positions, low, frac, features):
    return pl.pallas_call(
        structure_kernel,
        out_shape=(
            jax.ShapeDtypeStruct((2 * USED, ATOMS), jnp.bfloat16),
            jax.ShapeDtypeStruct((8, ATOMS), jnp.float32),
            jax.ShapeDtypeStruct((HALF, COLS), jnp.float32),
            jax.ShapeDtypeStruct((HALF, COLS), jnp.bfloat16),
        ),
        in_specs=[smem, hbm, hbm, hbm, hbm],
        out_specs=(hbm, vmem, vmem, vmem),
        scratch_shapes=[
            pltpu.VMEM((2 * USED, ATOMS), jnp.bfloat16),
            pltpu.VMEM((ATOMS, COLS), jnp.bfloat16),
            pltpu.VMEM((2, ATOMS), jnp.float32),
            pltpu.VMEM((1, ATOMS), jnp.int32),
            pltpu.VMEM((1, ATOMS), jnp.float32),
            pltpu.VMEM((ATOMS, CHAN), jnp.float32),
            pltpu.SemaphoreType.DMA((4,)),
            pltpu.SemaphoreType.DMA,
        ],
        cost_estimate=cost(1_500_000_000, 8_000_000),
        compiler_params=params(60),
        name="local_structure",
    )(meta, positions, low, frac, features)


def wave_square(half, chunk):
    place = lax.broadcasted_iota(jnp.int32, (CHUNK, CHAN), 0)
    n = 6 * half + 1 + (place >> 2)
    n_square = jnp.where(chunk <= 12, n * n, 0)
    a_square = jnp.where(chunk < 12, (chunk + 1) * (chunk + 1), 0)
    return (n_square + a_square).astype(jnp.float32)


def coefficient_kernel(meta, waves, filters, alpha, beta):
    half, chunk = meta[0], meta[1]
    place = lax.broadcasted_iota(jnp.int32, (CHUNK, 512), 0)
    role = place & 3
    n = 6 * half + 1 + (place >> 2)
    along_x = (role == 1) | (role == 2)
    only_zero = jnp.where((place == 0) & (chunk == 13) & (half == 0), 0, -1)
    a = jnp.where(chunk < 12, chunk + 1, jnp.where(chunk == 12, jnp.where(along_x, n, 0), only_zero))
    b = jnp.where(chunk < 12, n, jnp.where(chunk == 12, jnp.where(along_x, 0, n), only_zero))
    kx, ky = waves[0:1, :], waves[1:2, :]
    hit = jnp.where((jnp.abs(kx) == a) & (jnp.abs(ky) == b), 1.0, 0.0)
    product = kx * ky
    sign = jnp.where(product > 0, 1.0, jnp.where(product < 0, -1.0, 0.0))
    signed = hit * sign * jnp.where(role < 2, -1.0, 1.0)
    both = jnp.dot(
        jnp.concatenate([hit, signed], axis=0),
        filters[...],
        preferred_element_type=jnp.float32,
        precision=lax.Precision.HIGHEST,
    )
    alpha[...] = both[0:CHUNK]
    beta[...] = both[CHUNK : 2 * CHUNK]


def coefficients(meta, waves, filters):
    return pl.pallas_call(
        coefficient_kernel,
        out_shape=(jax.ShapeDtypeStruct((CHUNK, CHAN), jnp.float32),) * 2,
        in_specs=[smem, vmem, vmem],
        out_specs=(vmem, vmem),
        cost_estimate=cost(40_000_000, 300_000),
        compiler_params=params(),
        name="coefficients",
    )(meta, waves, filters)


def spatial_wave(square, screen):
    return jnp.sqrt((two_pi * two_pi) * square + screen * screen)


def source_kernel(meta, screening, parts, source, payload):
    total = parts[0].astype(jnp.float32)
    for at in range(1, CHUNKS):
        total = total + parts[at].astype(jnp.float32)
    total = total * float(ATOMS * XY_DEVICES) ** -0.5
    source[...] = total
    square = wave_square(meta[0], meta[1])
    decay = [
        jnp.exp(-plane_gap * spatial_wave(square, screening[plane])) for plane in range(PLANES)
    ]
    planes = [total[:, plane * CHAN : (plane + 1) * CHAN] for plane in range(PLANES)]
    upward = planes[0]
    for plane in range(1, PLANES):
        upward = decay[plane] * upward + planes[plane]
    downward = planes[PLANES - 1]
    for plane in reversed(range(PLANES - 1)):
        downward = decay[plane] * downward + planes[plane]
    layer = meta[2]
    which = lax.broadcasted_iota(jnp.int32, (8, CHAN), 0)
    screens = jnp.zeros((8, CHAN), jnp.float32)
    for plane in range(PLANES):
        screens = jnp.where(which == plane, screening[plane], screens)
    for target in range(LAYERS):
        payload[target, 0:CHUNK, :] = jnp.where(layer < target, upward, downward)
        payload[target, CHUNK:PAYLOAD, :] = screens


def local_source(meta, screening, parts):
    return pl.pallas_call(
        source_kernel,
        out_shape=(
            jax.ShapeDtypeStruct((CHUNK, COLS), jnp.float32),
            jax.ShapeDtypeStruct((LAYERS, PAYLOAD, CHAN), jnp.float32),
        ),
        in_specs=[smem, smem, vmem],
        out_specs=(vmem, vmem),
        cost_estimate=cost(1_000_000, 600_000),
        compiler_params=params(),
        name="local_source",
    )(meta, screening, parts)


def potential_kernel(meta, screening, source, carried, alpha, beta, out):
    square = wave_square(meta[0], meta[1])
    layer = meta[2]
    upward = jnp.zeros((CHUNK, CHAN), jnp.float32)
    downward = jnp.zeros((CHUNK, CHAN), jnp.float32)
    scales = []
    for at in range(LAYERS):
        depth = jnp.zeros((CHUNK, CHAN), jnp.float32)
        for plane in range(PLANES):
            depth = depth + spatial_wave(square, carried[at, CHUNK + plane : CHUNK + plane + 1, :])
        scales.append(jnp.exp(-plane_gap * depth))
    for at in range(LAYERS):
        upward = jnp.where(at < layer, scales[at] * upward + carried[at, 0:CHUNK, :], upward)
    for at in reversed(range(LAYERS)):
        downward = jnp.where(at > layer, scales[at] * downward + carried[at, 0:CHUNK, :], downward)
    spatial = [spatial_wave(square, screening[plane]) for plane in range(PLANES)]
    decay = [jnp.exp(-plane_gap * s) for s in spatial]
    planes = [source[:, plane * CHAN : (plane + 1) * CHAN] for plane in range(PLANES)]
    sums = []
    for plane in range(PLANES):
        upward = decay[plane] * upward + planes[plane]
        sums.append(upward - planes[plane])
    for plane in reversed(range(PLANES)):
        downward = decay[plane] * downward + planes[plane]
        sums[plane] = sums[plane] + downward
    odd = (lax.broadcasted_iota(jnp.int32, (CHUNK, CHAN), 0) & 1) == 1
    results = []
    for plane in range(PLANES):
        field = sums[plane]
        partner = jnp.where(odd, pltpu.roll(field, 1, 0), pltpu.roll(field, CHUNK - 1, 0))
        mixed = alpha[...] * field + beta[...] * partner
        results.append((long_gain * two_pi) / spatial[plane] * mixed)
    full = jnp.concatenate(results, axis=1).astype(jnp.bfloat16)
    for at in range(CHUNKS):
        out[at] = full


def local_potential(meta, screening, source, carried, alpha, beta):
    return pl.pallas_call(
        potential_kernel,
        out_shape=jax.ShapeDtypeStruct((CHUNKS, CHUNK, COLS), jnp.bfloat16),
        in_specs=[smem, smem, vmem, vmem, vmem, vmem],
        out_specs=vmem,
        cost_estimate=cost(1_000_000, 1_000_000),
        compiler_params=params(),
        name="local_potential",
    )(meta, screening, source, carried, alpha, beta)


def ghost_kernel(rows, features, sent, own, arrived):
    load = pltpu.make_async_copy(features, own, arrived)
    load.start()
    load.wait()

    def eight(at, _):
        for k in range(8):
            sent[at * 8 + k] = own[rows[at * 8 + k]]
        return 0

    lax.fori_loop(0, GHOST // 8, eight, 0)


def ghost_rows(rows, features):
    return pl.pallas_call(
        ghost_kernel,
        out_shape=(
            jax.ShapeDtypeStruct((GHOST, 1, CHAN), jnp.float32),
            jax.ShapeDtypeStruct((ATOMS, 1, CHAN), jnp.float32),
        ),
        in_specs=[smem, anywhere],
        out_specs=(vmem, vmem),
        scratch_shapes=[pltpu.SemaphoreType.DMA],
        cost_estimate=cost(1_000, 1_000_000),
        compiler_params=params(),
        name="ghost_rows",
    )(rows, features)


GROUP = 4
STEP = 8


def load_slots(neighbours, weight, slots, factors, arrived, first, count):
    copies = [
        pltpu.make_async_copy(neighbours.at[k, pl.ds(first, count)], slots[k], arrived.at[k])
        for k in range(NBR)
    ]
    copies.append(
        pltpu.make_async_copy(weight.at[:, pl.ds(first, count)], factors, arrived.at[NBR])
    )
    return copies


def weighted_rows(slots, factors, columns, table, sums, count):
    place = lax.broadcasted_iota(jnp.int32, (8, CHAN), 0)
    masks = [place == s for s in range(8)]
    tiles = 128 // GROUP

    def tile(at, _):
        lane = pl.multiple_of(at * 128, 128)
        block = factors[:, pl.ds(lane, 128)]
        for half in range(2):
            columns[:, half * GROUP : (half + 1) * GROUP, :] = jnp.transpose(
                block[half * 8 : half * 8 + 8]
            ).reshape(tiles, GROUP, 8)

        def step(inner, _):
            parts = []
            for g in range(STEP):
                group = inner * STEP + g
                atoms = [at * 128 + group * GROUP + j for j in range(GROUP)]
                factor = columns[group]
                total = None
                for k in range(8):
                    picked = None
                    for half in range(2):
                        for j in range(GROUP):
                            found = jnp.broadcast_to(
                                table[slots[k + 8 * half][atoms[j]]], (8, CHAN)
                            )
                            mask = masks[half * GROUP + j]
                            picked = found if picked is None else jnp.where(mask, found, picked)
                    term = picked * factor[:, k : k + 1]
                    total = term if total is None else total + term
                parts.append(total + pltpu.roll(total, GROUP, 0))
            for g in range(0, STEP, 2):
                row = pl.multiple_of(at * 128 + (inner * STEP + g) * GROUP, 8)
                sums[pl.ds(row, 8), :] = jnp.where(place < GROUP, parts[g], parts[g + 1])
            return 0

        return lax.fori_loop(0, tiles // STEP, step, 0)

    lax.fori_loop(0, count // 128, tile, 0)


def store_messages(sums, projection, short, out, stored, first, count):
    short[...] = jnp.dot(
        sums[...],
        projection[...],
        preferred_element_type=jnp.float32,
        precision=lax.Precision.HIGHEST,
    )
    copy = pltpu.make_async_copy(short, out.at[pl.ds(first, count)], stored)
    copy.start()
    copy.wait()


def pair_scratch(count):
    return [pltpu.SMEM((count,), jnp.int32)] * NBR + [
        pltpu.VMEM((NBR, count), jnp.float32),
        pltpu.VMEM((128 // GROUP, 8, 8), jnp.float32),
        pltpu.VMEM((count, CHAN), jnp.float32),
        pltpu.VMEM((count, CHAN), jnp.float32),
        pltpu.SemaphoreType.DMA((NBR + 1,)),
        pltpu.SemaphoreType.DMA,
    ]


def first_pairs(meta, neighbours, weight, w_short, features, sides, count):
    def kernel(meta, index, weights, projection, own, a, b, c, d, table, out, *scratch):
        slots = scratch[:NBR]
        factors, columns, sums, short, arrived, stored, placed = scratch[NBR:]
        loads = load_slots(index, weights, slots, factors, arrived, 0, count)
        core = meta[0]
        odd = meta[2] & 1
        loads.append(pltpu.make_async_copy(own, table.at[pl.ds(0, ATOMS)], placed.at[0]))
        for at, (rows, slot) in enumerate(
            ((a, 1 - core), (b, core), (c, 3 - odd), (d, 2 + odd))
        ):
            start = ATOMS + slot * GHOST
            loads.append(
                pltpu.make_async_copy(rows, table.at[pl.ds(start, GHOST)], placed.at[1 + at])
            )
        for load in loads:
            load.start()
        for load in loads:
            load.wait()
        weighted_rows(slots, factors, columns, table, sums, count)
        store_messages(sums, projection, short, out, stored, 0, count)

    return pl.pallas_call(
        kernel,
        out_shape=(
            jax.ShapeDtypeStruct((TABLE, 1, CHAN), jnp.float32),
            jax.ShapeDtypeStruct((ATOMS, CHAN), jnp.float32),
        ),
        in_specs=[smem, anywhere, anywhere, vmem] + [anywhere] * 5,
        out_specs=(vmem, anywhere),
        scratch_shapes=pair_scratch(count) + [pltpu.SemaphoreType.DMA((5,))],
        cost_estimate=cost(count * 200_000, count * 57_000),
        compiler_params=params(),
        name="first_pairs",
    )(meta, neighbours, weight, w_short, features, *sides)


def more_pairs(neighbours, weight, w_short, table, messages, first, count, name):
    def kernel(index, weights, projection, rows, before, out, *scratch):
        slots = scratch[:NBR]
        factors, columns, sums, short, arrived, stored = scratch[NBR:]
        loads = load_slots(index, weights, slots, factors, arrived, first, count)
        for load in loads:
            load.start()
        for load in loads:
            load.wait()
        weighted_rows(slots, factors, columns, rows, sums, count)
        store_messages(sums, projection, short, out, stored, first, count)

    return pl.pallas_call(
        kernel,
        out_shape=jax.ShapeDtypeStruct((ATOMS, CHAN), jnp.float32),
        in_specs=[anywhere, anywhere, vmem, vmem, anywhere],
        out_specs=anywhere,
        input_output_aliases={4: 0},
        scratch_shapes=pair_scratch(count),
        cost_estimate=cost(count * 200_000, count * 57_000),
        compiler_params=params(),
        name=name,
    )(neighbours, weight, w_short, table, messages)


def project_kernel(meta, mine, theirs, phase_in, hat, short, out, phase, arrived):
    at = pl.program_id(0)
    loads = [
        pltpu.make_async_copy(phase_in.at[:, pl.ds(i * BLOCK, BLOCK)], phase.at[i], arrived.at[i])
        for i in range(ATOMS // BLOCK)
    ]

    @pl.when(at == 0)
    def _():
        for load in loads:
            load.start()

    for i, load in enumerate(loads):

        @pl.when(at == i)
        def _():
            load.wait()

    atoms = pl.ds(pl.multiple_of(at * BLOCK, BLOCK), BLOCK)
    core = meta[0]
    dims = (((0,), (0,)), ((), ()))
    near = pl.multiple_of(core * USED, 16)
    far = pl.multiple_of((1 - core) * USED, 16)
    projected = lax.dot_general(
        mine[0:USED, :], phase[at, pl.ds(near, USED), :], dims, preferred_element_type=jnp.float32
    ) + lax.dot_general(
        theirs[0:USED, :], phase[at, pl.ds(far, USED), :], dims, preferred_element_type=jnp.float32
    )
    total = hat[0:1, atoms] * projected[0:CHAN]
    for plane in range(1, PLANES):
        total = total + hat[plane : plane + 1, atoms] * projected[plane * CHAN : (plane + 1) * CHAN]
    out[...] = jnp.transpose(total) + short[atoms, :]


def project(meta, mine, theirs, phase, hat, short):
    return pl.pallas_call(
        project_kernel,
        grid=(ATOMS // BLOCK,),
        out_shape=jax.ShapeDtypeStruct((ATOMS, CHAN), jnp.float32),
        in_specs=[smem, vmem, vmem, hbm, vmem, vmem],
        out_specs=pl.BlockSpec((BLOCK, CHAN), lambda i: (i, 0)),
        scratch_shapes=[
            pltpu.VMEM((ATOMS // BLOCK, 2 * USED, BLOCK), jnp.bfloat16),
            pltpu.SemaphoreType.DMA((ATOMS // BLOCK,)),
        ],
        cost_estimate=cost(1_500_000_000, 6_000_000),
        compiler_params=params(50),
        name="project",
    )(meta, mine, theirs, phase, hat, short)


PIECES = (512, 640, 896)


def swapped(value, axis, start):
    count = lax.axis_size(axis)
    ring = axis == LATERAL
    route = []
    for low in range(start, count, 2):
        if low + 1 < count or ring:
            high = (low + 1) % count
            route += [(low, high), (high, low)]
    return lax.ppermute(value, axis, route)


def other_core(value):
    return lax.ppermute(value, "core", [(0, 1), (1, 0)])


def on_device(
    features,
    positions,
    plane_index,
    plane_frac,
    neighbours,
    pair_weight,
    ghost_index,
    wave_index,
    channel_filter,
    screening,
    w_short,
):
    tie = lax.optimization_barrier
    meta = jnp.stack(
        [lax.axis_index("core"), lax.axis_index(SWAP), lax.axis_index(VERTICAL)]
    ).astype(jnp.int32)
    phase, hat, own, other = local_structure(
        meta, positions, plane_index.reshape(1, -1), plane_frac.reshape(1, -1), features
    )
    joined = (own + other_core(other).astype(jnp.float32)).astype(jnp.bfloat16)
    joined = joined.reshape(CHUNKS, CHUNK, COLS)
    joined, ghost_index = tie((joined, ghost_index))
    parts = lax.all_to_all(joined, SWAP, 0, 0)

    sent, own_rows = ghost_rows(ghost_index, features.reshape(ATOMS, 1, CHAN))
    sides = [
        swapped(sent, LATERAL, 0),
        swapped(sent, LATERAL, 1),
        swapped(sent, VERTICAL, 0),
        swapped(sent, VERTICAL, 1),
    ]
    alpha, beta = coefficients(meta, wave_index, channel_filter)
    first, second = PIECES[0], PIECES[0] + PIECES[1]
    table, short = first_pairs(meta, neighbours, pair_weight, w_short, own_rows, sides, first)

    parts, short, alpha, beta = tie((parts, short, alpha, beta))
    source, payload = local_source(meta, screening, parts)
    payload, short = tie((payload, short))
    carried = lax.all_to_all(payload, VERTICAL, 0, 0)
    short = more_pairs(
        neighbours, pair_weight, w_short, table, short, first, PIECES[1], "second_pairs"
    )

    carried, short = tie((carried, short))
    field = local_potential(meta, screening, source, carried, alpha, beta)
    field, short = tie((field, short))
    mine = lax.all_to_all(field, SWAP, 0, 0)
    short = more_pairs(
        neighbours, pair_weight, w_short, table, short, second, PIECES[2], "third_pairs"
    )

    mine, short = tie((mine, short))
    mine = mine.reshape(HALF, COLS)
    theirs = other_core(mine)
    return project(meta, mine, theirs, phase, hat, short)


def solution(mesh):
    split = Mesh(mesh.devices.reshape(8, 2, 2, 2, 4), SPLIT)
    return jax.shard_map(
        on_device,
        mesh=split,
        in_specs=(
            P(SPLIT, None),
            P(None, SPLIT),
            P(SPLIT),
            P(SPLIT),
            P(None, SPLIT),
            P(None, SPLIT),
            P(SPLIT),
            P(),
            P(),
            P(VERTICAL),
            P(),
        ),
        out_specs=P(SPLIT, None),
        check_vma=False,
    )
```

```python
import math

import jax
import jax.numpy as jnp
from jax import lax
from jax.experimental import pallas as pl
from jax.experimental.pallas import tpu as pltpu
from jax.sharding import Mesh
from jax.sharding import PartitionSpec as P

two_pi = 2.0 * math.pi
plane_gap = 0.01
long_gain = 0.125

ATOMS = 2048
CHAN = 128
PLANES = 4
COLS = PLANES * CHAN
NBR = 16
GHOST = 256
TABLE = ATOMS + 4 * GHOST
LAYERS = 8
XY_DEVICES = 32
CHUNK = 24
CHUNKS = 16
HALF = CHUNKS * CHUNK
USED = 14 * CHUNK
PAYLOAD = 32

SPLIT = ("z", "xl", "core", "xh", "y")
LATERAL = ("z", "xl", "core")
SWAP = ("z", "xl")
VERTICAL = ("xh", "y")

smem = pl.BlockSpec(memory_space=pltpu.SMEM)
vmem = pl.BlockSpec(memory_space=pltpu.VMEM)
anywhere = pl.BlockSpec(memory_space=pl.ANY)
hbm = pl.BlockSpec(memory_space=pltpu.HBM)


def cost(flops, nbytes):
    return pl.CostEstimate(flops=flops, bytes_accessed=nbytes, transcendentals=0)


def params(mebibytes=8):
    return pltpu.CompilerParams(vmem_limit_bytes=mebibytes << 20)


BLOCK = 512


def structure_kernel(
    meta,
    positions,
    plane_low,
    plane_height,
    features,
    phase_out,
    hat,
    own,
    other,
    phase,
    weighted,
    pos,
    low,
    frac,
    feat,
    arrived,
    kept,
):
    loads = [
        pltpu.make_async_copy(source, target, arrived.at[at])
        for at, (source, target) in enumerate(
            ((positions, pos), (plane_low, low), (plane_height, frac), (features, feat))
        )
    ]
    for load in loads:
        load.start()
    for load in loads:
        load.wait()
    keep = pltpu.make_async_copy(phase, phase_out, kept)
    tile_row = lax.broadcasted_iota(jnp.int32, (8, BLOCK), 0)
    upper = tile_row >= 4
    role = tile_row & 3
    wave_is_sin_x = (role == 1) | (role == 2)
    wave_is_sin_y = (role & 1) == 1
    orders = lax.broadcasted_iota(jnp.int32, (16, BLOCK), 0).astype(jnp.float32)

    def row(table, at):
        return jnp.broadcast_to(table[at : at + 1, :], (8, BLOCK))

    def block(at, _):
        lanes = pl.ds(pl.multiple_of(at * BLOCK, BLOCK), BLOCK)

        def tables(coordinate):
            turns = orders * coordinate
            turns = turns - jnp.floor(turns + 0.5)
            angle = two_pi * turns
            return jnp.cos(angle), jnp.sin(angle)

        cos_x, sin_x = tables(pos[0:1, lanes])
        cos_y, sin_y = tables(pos[1:2, lanes])
        for half in range(2):
            b_tiles, axis_tiles = [], []
            for tile in range(3):
                n = 6 * half + 1 + 2 * tile
                cos_n = jnp.where(upper, row(cos_y, n + 1), row(cos_y, n))
                sin_n = jnp.where(upper, row(sin_y, n + 1), row(sin_y, n))
                b_tiles.append(jnp.where(wave_is_sin_y, sin_n, cos_n))
                cos_m = jnp.where(upper, row(cos_x, n + 1), row(cos_x, n))
                sin_m = jnp.where(upper, row(sin_x, n + 1), row(sin_x, n))
                axis_tiles.append(
                    jnp.where(
                        role == 0,
                        cos_n,
                        jnp.where(role == 1, cos_m, jnp.where(role == 2, sin_m, sin_n)),
                    )
                )
            for pair in range(6):
                parts = []
                for a in (2 * pair + 1, 2 * pair + 2):
                    a_tile = jnp.where(wave_is_sin_x, row(sin_x, a), row(cos_x, a))
                    parts += [a_tile * b_tile for b_tile in b_tiles]
                rows = half * USED + pair * 2 * CHUNK
                phase[rows : rows + 2 * CHUNK, lanes] = jnp.concatenate(parts, axis=0).astype(
                    jnp.bfloat16
                )
            zero = jnp.zeros((8, BLOCK), jnp.float32)
            first = jnp.where(tile_row == 0, 1.0, 0.0) if half == 0 else zero
            rows = half * USED + 12 * CHUNK
            phase[rows : rows + 2 * CHUNK, lanes] = jnp.concatenate(
                axis_tiles + [first, zero, zero], axis=0
            ).astype(jnp.bfloat16)

        low_plane = low[:, lanes]
        height = frac[:, lanes]
        hat_block = jnp.where(tile_row == low_plane, 1.0 - height, 0.0) + jnp.where(
            tile_row == low_plane + 1, height, 0.0
        )
        hat[:, lanes] = hat_block
        hat_cols = jnp.transpose(hat_block)
        feat_block = feat[lanes, :]
        for plane in range(PLANES):
            weighted[lanes, plane * CHAN : (plane + 1) * CHAN] = (
                hat_cols[:, plane : plane + 1] * feat_block
            ).astype(jnp.bfloat16)
        return 0

    lax.fori_loop(0, ATOMS // BLOCK, block, 0)
    keep.start()
    core = meta[0]
    for mine in (False, True):
        start = pl.multiple_of((core if mine else 1 - core) * USED, 16)
        sums = jnp.dot(
            phase[pl.ds(start, USED), :], weighted[...], preferred_element_type=jnp.float32
        )
        rest = jnp.zeros((HALF - USED, COLS), jnp.float32)
        if mine:
            own[0:USED, :] = sums
            own[USED:HALF, :] = rest
        else:
            other[0:USED, :] = sums.astype(jnp.bfloat16)
            other[USED:HALF, :] = rest.astype(jnp.bfloat16)
    keep.wait()


def local_structure(meta, positions, low, frac, features):
    return pl.pallas_call(
        structure_kernel,
        out_shape=(
            jax.ShapeDtypeStruct((2 * USED, ATOMS), jnp.bfloat16),
            jax.ShapeDtypeStruct((8, ATOMS), jnp.float32),
            jax.ShapeDtypeStruct((HALF, COLS), jnp.float32),
            jax.ShapeDtypeStruct((HALF, COLS), jnp.bfloat16),
        ),
        in_specs=[smem, hbm, hbm, hbm, hbm],
        out_specs=(hbm, vmem, vmem, vmem),
        scratch_shapes=[
            pltpu.VMEM((2 * USED, ATOMS), jnp.bfloat16),
            pltpu.VMEM((ATOMS, COLS), jnp.bfloat16),
            pltpu.VMEM((2, ATOMS), jnp.float32),
            pltpu.VMEM((1, ATOMS), jnp.int32),
            pltpu.VMEM((1, ATOMS), jnp.float32),
            pltpu.VMEM((ATOMS, CHAN), jnp.float32),
            pltpu.SemaphoreType.DMA((4,)),
            pltpu.SemaphoreType.DMA,
        ],
        cost_estimate=cost(1_500_000_000, 8_000_000),
        compiler_params=params(60),
        name="local_structure",
    )(meta, positions, low, frac, features)


def wave_square(half, chunk):
    place = lax.broadcasted_iota(jnp.int32, (CHUNK, CHAN), 0)
    n = 6 * half + 1 + (place >> 2)
    n_square = jnp.where(chunk <= 12, n * n, 0)
    a_square = jnp.where(chunk < 12, (chunk + 1) * (chunk + 1), 0)
    return (n_square + a_square).astype(jnp.float32)


def coefficient_kernel(meta, waves, filters, alpha, beta):
    half, chunk = meta[0], meta[1]
    place = lax.broadcasted_iota(jnp.int32, (CHUNK, 512), 0)
    role = place & 3
    n = 6 * half + 1 + (place >> 2)
    along_x = (role == 1) | (role == 2)
    only_zero = jnp.where((place == 0) & (chunk == 13) & (half == 0), 0, -1)
    a = jnp.where(chunk < 12, chunk + 1, jnp.where(chunk == 12, jnp.where(along_x, n, 0), only_zero))
    b = jnp.where(chunk < 12, n, jnp.where(chunk == 12, jnp.where(along_x, 0, n), only_zero))
    kx, ky = waves[0:1, :], waves[1:2, :]
    hit = jnp.where((jnp.abs(kx) == a) & (jnp.abs(ky) == b), 1.0, 0.0)
    product = kx * ky
    sign = jnp.where(product > 0, 1.0, jnp.where(product < 0, -1.0, 0.0))
    signed = hit * sign * jnp.where(role < 2, -1.0, 1.0)
    both = jnp.dot(
        jnp.concatenate([hit, signed], axis=0),
        filters[...],
        preferred_element_type=jnp.float32,
        precision=lax.Precision.HIGHEST,
    )
    alpha[...] = both[0:CHUNK]
    beta[...] = both[CHUNK : 2 * CHUNK]


def coefficients(meta, waves, filters):
    return pl.pallas_call(
        coefficient_kernel,
        out_shape=(jax.ShapeDtypeStruct((CHUNK, CHAN), jnp.float32),) * 2,
        in_specs=[smem, vmem, vmem],
        out_specs=(vmem, vmem),
        cost_estimate=cost(40_000_000, 300_000),
        compiler_params=params(),
        name="coefficients",
    )(meta, waves, filters)


def spatial_wave(square, screen):
    return jnp.sqrt((two_pi * two_pi) * square + screen * screen)


def source_kernel(meta, screening, parts, source, payload):
    total = parts[0].astype(jnp.float32)
    for at in range(1, CHUNKS):
        total = total + parts[at].astype(jnp.float32)
    total = total * float(ATOMS * XY_DEVICES) ** -0.5
    source[...] = total
    square = wave_square(meta[0], meta[1])
    decay = [
        jnp.exp(-plane_gap * spatial_wave(square, screening[plane])) for plane in range(PLANES)
    ]
    planes = [total[:, plane * CHAN : (plane + 1) * CHAN] for plane in range(PLANES)]
    upward = planes[0]
    for plane in range(1, PLANES):
        upward = decay[plane] * upward + planes[plane]
    downward = planes[PLANES - 1]
    for plane in reversed(range(PLANES - 1)):
        downward = decay[plane] * downward + planes[plane]
    layer = meta[2]
    which = lax.broadcasted_iota(jnp.int32, (8, CHAN), 0)
    screens = jnp.zeros((8, CHAN), jnp.float32)
    for plane in range(PLANES):
        screens = jnp.where(which == plane, screening[plane], screens)
    for target in range(LAYERS):
        payload[target, 0:CHUNK, :] = jnp.where(layer < target, upward, downward)
        payload[target, CHUNK:PAYLOAD, :] = screens


def local_source(meta, screening, parts):
    return pl.pallas_call(
        source_kernel,
        out_shape=(
            jax.ShapeDtypeStruct((CHUNK, COLS), jnp.float32),
            jax.ShapeDtypeStruct((LAYERS, PAYLOAD, CHAN), jnp.float32),
        ),
        in_specs=[smem, smem, vmem],
        out_specs=(vmem, vmem),
        cost_estimate=cost(1_000_000, 600_000),
        compiler_params=params(),
        name="local_source",
    )(meta, screening, parts)


def potential_kernel(meta, screening, source, carried, alpha, beta, out):
    square = wave_square(meta[0], meta[1])
    layer = meta[2]
    upward = jnp.zeros((CHUNK, CHAN), jnp.float32)
    downward = jnp.zeros((CHUNK, CHAN), jnp.float32)
    scales = []
    for at in range(LAYERS):
        depth = jnp.zeros((CHUNK, CHAN), jnp.float32)
        for plane in range(PLANES):
            depth = depth + spatial_wave(square, carried[at, CHUNK + plane : CHUNK + plane + 1, :])
        scales.append(jnp.exp(-plane_gap * depth))
    for at in range(LAYERS):
        upward = jnp.where(at < layer, scales[at] * upward + carried[at, 0:CHUNK, :], upward)
    for at in reversed(range(LAYERS)):
        downward = jnp.where(at > layer, scales[at] * downward + carried[at, 0:CHUNK, :], downward)
    spatial = [spatial_wave(square, screening[plane]) for plane in range(PLANES)]
    decay = [jnp.exp(-plane_gap * s) for s in spatial]
    planes = [source[:, plane * CHAN : (plane + 1) * CHAN] for plane in range(PLANES)]
    sums = []
    for plane in range(PLANES):
        upward = decay[plane] * upward + planes[plane]
        sums.append(upward - planes[plane])
    for plane in reversed(range(PLANES)):
        downward = decay[plane] * downward + planes[plane]
        sums[plane] = sums[plane] + downward
    odd = (lax.broadcasted_iota(jnp.int32, (CHUNK, CHAN), 0) & 1) == 1
    results = []
    for plane in range(PLANES):
        field = sums[plane]
        partner = jnp.where(odd, pltpu.roll(field, 1, 0), pltpu.roll(field, CHUNK - 1, 0))
        mixed = alpha[...] * field + beta[...] * partner
        results.append((long_gain * two_pi) / spatial[plane] * mixed)
    full = jnp.concatenate(results, axis=1).astype(jnp.bfloat16)
    for at in range(CHUNKS):
        out[at] = full


def local_potential(meta, screening, source, carried, alpha, beta):
    return pl.pallas_call(
        potential_kernel,
        out_shape=jax.ShapeDtypeStruct((CHUNKS, CHUNK, COLS), jnp.bfloat16),
        in_specs=[smem, smem, vmem, vmem, vmem, vmem],
        out_specs=vmem,
        cost_estimate=cost(1_000_000, 1_000_000),
        compiler_params=params(),
        name="local_potential",
    )(meta, screening, source, carried, alpha, beta)


def ghost_kernel(rows, features, sent, own, arrived):
    load = pltpu.make_async_copy(features, own, arrived)
    load.start()
    load.wait()

    def eight(at, _):
        for k in range(8):
            sent[at * 8 + k] = own[rows[at * 8 + k]]
        return 0

    lax.fori_loop(0, GHOST // 8, eight, 0)


def ghost_rows(rows, features):
    return pl.pallas_call(
        ghost_kernel,
        out_shape=(
            jax.ShapeDtypeStruct((GHOST, 1, CHAN), jnp.float32),
            jax.ShapeDtypeStruct((ATOMS, 1, CHAN), jnp.float32),
        ),
        in_specs=[smem, anywhere],
        out_specs=(vmem, vmem),
        scratch_shapes=[pltpu.SemaphoreType.DMA],
        cost_estimate=cost(1_000, 1_000_000),
        compiler_params=params(),
        name="ghost_rows",
    )(rows, features)


GROUP = 4
STEP = 8


def load_slots(neighbours, weight, slots, factors, arrived, first, count):
    quarter = count // GROUP
    copies = [
        pltpu.make_async_copy(
            neighbours.at[k, pl.ds(first + j * quarter, quarter)],
            slots[k * GROUP + j],
            arrived.at[k * GROUP + j],
        )
        for k in range(NBR)
        for j in range(GROUP)
    ]
    copies.append(
        pltpu.make_async_copy(
            weight.at[:, pl.ds(first, count)], factors, arrived.at[NBR * GROUP]
        )
    )
    return copies


def weighted_rows(slots, factors, columns, table, sums, count):
    quarter = count // GROUP
    place = lax.broadcasted_iota(jnp.int32, (8, CHAN), 0)
    masks = [place == s for s in range(8)]
    for j in range(GROUP):
        for half in range(2):
            columns[:, half * GROUP + j, :] = jnp.transpose(
                factors[half * 8 : half * 8 + 8, j * quarter : (j + 1) * quarter]
            )

    def step(at, _):
        for g in range(STEP):
            group = at * STEP + g
            factor = columns[group]
            total = None
            for k in range(8):
                picked = None
                for half in range(2):
                    for j in range(GROUP):
                        row = slots[(k + 8 * half) * GROUP + j][group]
                        found = jnp.broadcast_to(table[row], (8, CHAN))
                        mask = masks[half * GROUP + j]
                        picked = found if picked is None else jnp.where(mask, found, picked)
                term = picked * factor[:, k : k + 1]
                total = term if total is None else total + term
            total = total + pltpu.roll(total, GROUP, 0)
            sums[pl.ds(group, GROUP, stride=quarter), :] = total[0:GROUP]
        return 0

    lax.fori_loop(0, quarter // STEP, step, 0)


def store_messages(sums, projection, short, out, stored, first, count):
    short[...] = jnp.dot(
        sums[...],
        projection[...],
        preferred_element_type=jnp.float32,
        precision=lax.Precision.HIGHEST,
    )
    copy = pltpu.make_async_copy(short, out.at[pl.ds(first, count)], stored)
    copy.start()
    copy.wait()


def pair_scratch(count):
    return [pltpu.SMEM((count // GROUP,), jnp.int32)] * (NBR * GROUP) + [
        pltpu.VMEM((NBR, count), jnp.float32),
        pltpu.VMEM((count // GROUP, 8, 8), jnp.float32),
        pltpu.VMEM((count, CHAN), jnp.float32),
        pltpu.VMEM((count, CHAN), jnp.float32),
        pltpu.SemaphoreType.DMA((NBR * GROUP + 1,)),
        pltpu.SemaphoreType.DMA,
    ]


def first_pairs(meta, neighbours, weight, w_short, features, sides, count):
    def kernel(meta, index, weights, projection, own, a, b, c, d, table, out, *scratch):
        slots = scratch[: NBR * GROUP]
        factors, columns, sums, short, arrived, stored, placed = scratch[NBR * GROUP :]
        loads = load_slots(index, weights, slots, factors, arrived, 0, count)
        core = meta[0]
        odd = meta[2] & 1
        loads.append(pltpu.make_async_copy(own, table.at[pl.ds(0, ATOMS)], placed.at[0]))
        for at, (rows, slot) in enumerate(
            ((a, 1 - core), (b, core), (c, 3 - odd), (d, 2 + odd))
        ):
            start = ATOMS + slot * GHOST
            loads.append(
                pltpu.make_async_copy(rows, table.at[pl.ds(start, GHOST)], placed.at[1 + at])
            )
        for load in loads:
            load.start()
        for load in loads:
            load.wait()
        weighted_rows(slots, factors, columns, table, sums, count)
        store_messages(sums, projection, short, out, stored, 0, count)

    return pl.pallas_call(
        kernel,
        out_shape=(
            jax.ShapeDtypeStruct((TABLE, 1, CHAN), jnp.float32),
            jax.ShapeDtypeStruct((ATOMS, CHAN), jnp.float32),
        ),
        in_specs=[smem, anywhere, anywhere, vmem] + [anywhere] * 5,
        out_specs=(vmem, anywhere),
        scratch_shapes=pair_scratch(count) + [pltpu.SemaphoreType.DMA((5,))],
        cost_estimate=cost(count * 200_000, count * 57_000),
        compiler_params=params(),
        name="first_pairs",
    )(meta, neighbours, weight, w_short, features, *sides)


def more_pairs(neighbours, weight, w_short, table, messages, first, count, name):
    def kernel(index, weights, projection, rows, before, out, *scratch):
        slots = scratch[: NBR * GROUP]
        factors, columns, sums, short, arrived, stored = scratch[NBR * GROUP :]
        loads = load_slots(index, weights, slots, factors, arrived, first, count)
        for load in loads:
            load.start()
        for load in loads:
            load.wait()
        weighted_rows(slots, factors, columns, rows, sums, count)
        store_messages(sums, projection, short, out, stored, first, count)

    return pl.pallas_call(
        kernel,
        out_shape=jax.ShapeDtypeStruct((ATOMS, CHAN), jnp.float32),
        in_specs=[anywhere, anywhere, vmem, vmem, anywhere],
        out_specs=anywhere,
        input_output_aliases={4: 0},
        scratch_shapes=pair_scratch(count),
        cost_estimate=cost(count * 200_000, count * 57_000),
        compiler_params=params(),
        name=name,
    )(neighbours, weight, w_short, table, messages)


def project_kernel(meta, mine, theirs, phase_in, hat, short, out, phase, arrived):
    at = pl.program_id(0)
    loads = [
        pltpu.make_async_copy(phase_in.at[:, pl.ds(i * BLOCK, BLOCK)], phase.at[i], arrived.at[i])
        for i in range(ATOMS // BLOCK)
    ]

    @pl.when(at == 0)
    def _():
        for load in loads:
            load.start()

    for i, load in enumerate(loads):

        @pl.when(at == i)
        def _():
            load.wait()

    atoms = pl.ds(pl.multiple_of(at * BLOCK, BLOCK), BLOCK)
    core = meta[0]
    dims = (((0,), (0,)), ((), ()))
    near = pl.multiple_of(core * USED, 16)
    far = pl.multiple_of((1 - core) * USED, 16)
    projected = lax.dot_general(
        mine[0:USED, :], phase[at, pl.ds(near, USED), :], dims, preferred_element_type=jnp.float32
    ) + lax.dot_general(
        theirs[0:USED, :], phase[at, pl.ds(far, USED), :], dims, preferred_element_type=jnp.float32
    )
    total = hat[0:1, atoms] * projected[0:CHAN]
    for plane in range(1, PLANES):
        total = total + hat[plane : plane + 1, atoms] * projected[plane * CHAN : (plane + 1) * CHAN]
    out[...] = jnp.transpose(total) + short[atoms, :]


def project(meta, mine, theirs, phase, hat, short):
    return pl.pallas_call(
        project_kernel,
        grid=(ATOMS // BLOCK,),
        out_shape=jax.ShapeDtypeStruct((ATOMS, CHAN), jnp.float32),
        in_specs=[smem, vmem, vmem, hbm, vmem, vmem],
        out_specs=pl.BlockSpec((BLOCK, CHAN), lambda i: (i, 0)),
        scratch_shapes=[
            pltpu.VMEM((ATOMS // BLOCK, 2 * USED, BLOCK), jnp.bfloat16),
            pltpu.SemaphoreType.DMA((ATOMS // BLOCK,)),
        ],
        cost_estimate=cost(1_500_000_000, 6_000_000),
        compiler_params=params(50),
        name="project",
    )(meta, mine, theirs, phase, hat, short)


PIECES = (512, 512, 1024)


def swapped(value, axis, start):
    count = lax.axis_size(axis)
    ring = axis == LATERAL
    route = []
    for low in range(start, count, 2):
        if low + 1 < count or ring:
            high = (low + 1) % count
            route += [(low, high), (high, low)]
    return lax.ppermute(value, axis, route)


def other_core(value):
    return lax.ppermute(value, "core", [(0, 1), (1, 0)])


def on_device(
    features,
    positions,
    plane_index,
    plane_frac,
    neighbours,
    pair_weight,
    ghost_index,
    wave_index,
    channel_filter,
    screening,
    w_short,
):
    tie = lax.optimization_barrier
    meta = jnp.stack(
        [lax.axis_index("core"), lax.axis_index(SWAP), lax.axis_index(VERTICAL)]
    ).astype(jnp.int32)
    phase, hat, own, other = local_structure(
        meta, positions, plane_index.reshape(1, -1), plane_frac.reshape(1, -1), features
    )
    joined = (own + other_core(other).astype(jnp.float32)).astype(jnp.bfloat16)
    joined = joined.reshape(CHUNKS, CHUNK, COLS)
    joined, ghost_index = tie((joined, ghost_index))
    parts = lax.all_to_all(joined, SWAP, 0, 0)

    sent, own_rows = ghost_rows(ghost_index, features.reshape(ATOMS, 1, CHAN))
    sides = [
        swapped(sent, LATERAL, 0),
        swapped(sent, LATERAL, 1),
        swapped(sent, VERTICAL, 0),
        swapped(sent, VERTICAL, 1),
    ]
    alpha, beta = coefficients(meta, wave_index, channel_filter)
    first, second = PIECES[0], PIECES[0] + PIECES[1]
    table, short = first_pairs(meta, neighbours, pair_weight, w_short, own_rows, sides, first)

    parts, short, alpha, beta = tie((parts, short, alpha, beta))
    source, payload = local_source(meta, screening, parts)
    payload, short = tie((payload, short))
    carried = lax.all_to_all(payload, VERTICAL, 0, 0)
    short = more_pairs(
        neighbours, pair_weight, w_short, table, short, first, PIECES[1], "second_pairs"
    )

    carried, short = tie((carried, short))
    field = local_potential(meta, screening, source, carried, alpha, beta)
    field, short = tie((field, short))
    mine = lax.all_to_all(field, SWAP, 0, 0)
    short = more_pairs(
        neighbours, pair_weight, w_short, table, short, second, PIECES[2], "third_pairs"
    )

    mine, short = tie((mine, short))
    mine = mine.reshape(HALF, COLS)
    theirs = other_core(mine)
    return project(meta, mine, theirs, phase, hat, short)


def solution(mesh):
    split = Mesh(mesh.devices.reshape(8, 2, 2, 2, 4), SPLIT)
    return jax.shard_map(
        on_device,
        mesh=split,
        in_specs=(
            P(SPLIT, None),
            P(None, SPLIT),
            P(SPLIT),
            P(SPLIT),
            P(None, SPLIT),
            P(None, SPLIT),
            P(SPLIT),
            P(),
            P(),
            P(VERTICAL),
            P(),
        ),
        out_specs=P(SPLIT, None),
        check_vma=False,
    )
```

```python
import math

import jax
import jax.numpy as jnp
from jax import lax
from jax.experimental import pallas as pl
from jax.experimental.pallas import tpu as pltpu
from jax.sharding import Mesh
from jax.sharding import PartitionSpec as P

two_pi = 2.0 * math.pi
plane_gap = 0.01
long_gain = 0.125

ATOMS = 2048
CHAN = 128
PLANES = 4
COLS = PLANES * CHAN
NBR = 16
GHOST = 256
TABLE = ATOMS + 4 * GHOST
LAYERS = 8
XY_DEVICES = 32
CHUNK = 24
CHUNKS = 16
HALF = CHUNKS * CHUNK
USED = 14 * CHUNK
PAYLOAD = 32

SPLIT = ("z", "xl", "core", "xh", "y")
LATERAL = ("z", "xl", "core")
SWAP = ("z", "xl")
VERTICAL = ("xh", "y")

smem = pl.BlockSpec(memory_space=pltpu.SMEM)
vmem = pl.BlockSpec(memory_space=pltpu.VMEM)
anywhere = pl.BlockSpec(memory_space=pl.ANY)
hbm = pl.BlockSpec(memory_space=pltpu.HBM)


def cost(flops, nbytes):
    return pl.CostEstimate(flops=flops, bytes_accessed=nbytes, transcendentals=0)


def params(mebibytes=8):
    return pltpu.CompilerParams(vmem_limit_bytes=mebibytes << 20)


BLOCK = 512


def structure_kernel(
    positions,
    plane_low,
    plane_height,
    features,
    phase_out,
    hat,
    own,
    other,
    phase,
    weighted,
    pos,
    low,
    frac,
    feat,
    arrived,
    kept,
):
    loads = [
        pltpu.make_async_copy(source, target, arrived.at[at])
        for at, (source, target) in enumerate(
            ((positions, pos), (plane_low, low), (plane_height, frac), (features, feat))
        )
    ]
    for load in loads:
        load.start()
    for load in loads:
        load.wait()
    keep = pltpu.make_async_copy(phase, phase_out, kept)
    tile_row = lax.broadcasted_iota(jnp.int32, (8, BLOCK), 0)
    upper = tile_row >= 4
    role = tile_row & 3
    wave_is_sin_x = (role == 1) | (role == 2)
    wave_is_sin_y = (role & 1) == 1
    orders = lax.broadcasted_iota(jnp.int32, (16, BLOCK), 0).astype(jnp.float32)

    def row(table, at):
        return jnp.broadcast_to(table[at : at + 1, :], (8, BLOCK))

    def block(at, _):
        lanes = pl.ds(pl.multiple_of(at * BLOCK, BLOCK), BLOCK)

        def tables(coordinate):
            turns = orders * coordinate
            turns = turns - jnp.floor(turns + 0.5)
            angle = two_pi * turns
            return jnp.cos(angle), jnp.sin(angle)

        cos_x, sin_x = tables(pos[0:1, lanes])
        cos_y, sin_y = tables(pos[1:2, lanes])
        for half in range(2):
            b_tiles, axis_tiles = [], []
            for tile in range(3):
                n = 6 * half + 1 + 2 * tile
                cos_n = jnp.where(upper, row(cos_y, n + 1), row(cos_y, n))
                sin_n = jnp.where(upper, row(sin_y, n + 1), row(sin_y, n))
                b_tiles.append(jnp.where(wave_is_sin_y, sin_n, cos_n))
                cos_m = jnp.where(upper, row(cos_x, n + 1), row(cos_x, n))
                sin_m = jnp.where(upper, row(sin_x, n + 1), row(sin_x, n))
                axis_tiles.append(
                    jnp.where(
                        role == 0,
                        cos_n,
                        jnp.where(role == 1, cos_m, jnp.where(role == 2, sin_m, sin_n)),
                    )
                )
            for pair in range(6):
                parts = []
                for a in (2 * pair + 1, 2 * pair + 2):
                    a_tile = jnp.where(wave_is_sin_x, row(sin_x, a), row(cos_x, a))
                    parts += [a_tile * b_tile for b_tile in b_tiles]
                rows = half * USED + pair * 2 * CHUNK
                phase[rows : rows + 2 * CHUNK, lanes] = jnp.concatenate(parts, axis=0).astype(
                    jnp.bfloat16
                )
            zero = jnp.zeros((8, BLOCK), jnp.float32)
            first = jnp.where(tile_row == 0, 1.0, 0.0) if half == 0 else zero
            rows = half * USED + 12 * CHUNK
            phase[rows : rows + 2 * CHUNK, lanes] = jnp.concatenate(
                axis_tiles + [first, zero, zero], axis=0
            ).astype(jnp.bfloat16)

        low_plane = low[:, lanes]
        height = frac[:, lanes]
        hat_block = jnp.where(tile_row == low_plane, 1.0 - height, 0.0) + jnp.where(
            tile_row == low_plane + 1, height, 0.0
        )
        hat[:, lanes] = hat_block
        hat_cols = jnp.transpose(hat_block)
        feat_block = feat[lanes, :]
        for plane in range(PLANES):
            weighted[lanes, plane * CHAN : (plane + 1) * CHAN] = (
                hat_cols[:, plane : plane + 1] * feat_block
            ).astype(jnp.bfloat16)
        return 0

    lax.fori_loop(0, ATOMS // BLOCK, block, 0)
    keep.start()
    core = lax.axis_index("core")
    for mine in (False, True):
        start = pl.multiple_of((core if mine else 1 - core) * USED, 16)
        sums = jnp.dot(
            phase[pl.ds(start, USED), :], weighted[...], preferred_element_type=jnp.float32
        )
        rest = jnp.zeros((HALF - USED, COLS), jnp.float32)
        if mine:
            own[0:USED, :] = sums
            own[USED:HALF, :] = rest
        else:
            other[0:USED, :] = sums.astype(jnp.bfloat16)
            other[USED:HALF, :] = rest.astype(jnp.bfloat16)
    keep.wait()


def local_structure(positions, low, frac, features):
    return pl.pallas_call(
        structure_kernel,
        out_shape=(
            jax.ShapeDtypeStruct((2 * USED, ATOMS), jnp.bfloat16),
            jax.ShapeDtypeStruct((8, ATOMS), jnp.float32),
            jax.ShapeDtypeStruct((HALF, COLS), jnp.float32),
            jax.ShapeDtypeStruct((HALF, COLS), jnp.bfloat16),
        ),
        in_specs=[hbm, hbm, hbm, hbm],
        out_specs=(hbm, vmem, vmem, vmem),
        scratch_shapes=[
            pltpu.VMEM((2 * USED, ATOMS), jnp.bfloat16),
            pltpu.VMEM((ATOMS, COLS), jnp.bfloat16),
            pltpu.VMEM((2, ATOMS), jnp.float32),
            pltpu.VMEM((1, ATOMS), jnp.int32),
            pltpu.VMEM((1, ATOMS), jnp.float32),
            pltpu.VMEM((ATOMS, CHAN), jnp.float32),
            pltpu.SemaphoreType.DMA((4,)),
            pltpu.SemaphoreType.DMA,
        ],
        cost_estimate=cost(1_500_000_000, 8_000_000),
        compiler_params=params(60),
        name="local_structure",
    )(positions, low, frac, features)


def wave_square(half, chunk):
    place = lax.broadcasted_iota(jnp.int32, (CHUNK, CHAN), 0)
    n = 6 * half + 1 + (place >> 2)
    n_square = jnp.where(chunk <= 12, n * n, 0)
    a_square = jnp.where(chunk < 12, (chunk + 1) * (chunk + 1), 0)
    return (n_square + a_square).astype(jnp.float32)


def coefficient_kernel(waves, filters, alpha, beta):
    half, chunk = lax.axis_index("core"), lax.axis_index(SWAP)
    place = lax.broadcasted_iota(jnp.int32, (CHUNK, 512), 0)
    role = place & 3
    n = 6 * half + 1 + (place >> 2)
    along_x = (role == 1) | (role == 2)
    only_zero = jnp.where((place == 0) & (chunk == 13) & (half == 0), 0, -1)
    a = jnp.where(chunk < 12, chunk + 1, jnp.where(chunk == 12, jnp.where(along_x, n, 0), only_zero))
    b = jnp.where(chunk < 12, n, jnp.where(chunk == 12, jnp.where(along_x, 0, n), only_zero))
    kx, ky = waves[0:1, :], waves[1:2, :]
    hit = jnp.where((jnp.abs(kx) == a) & (jnp.abs(ky) == b), 1.0, 0.0)
    product = kx * ky
    sign = jnp.where(product > 0, 1.0, jnp.where(product < 0, -1.0, 0.0))
    signed = hit * sign * jnp.where(role < 2, -1.0, 1.0)
    both = jnp.dot(
        jnp.concatenate([hit, signed], axis=0),
        filters[...],
        preferred_element_type=jnp.float32,
        precision=lax.Precision.HIGHEST,
    )
    alpha[...] = both[0:CHUNK]
    beta[...] = both[CHUNK : 2 * CHUNK]


def coefficients(waves, filters):
    return pl.pallas_call(
        coefficient_kernel,
        out_shape=(jax.ShapeDtypeStruct((CHUNK, CHAN), jnp.float32),) * 2,
        in_specs=[vmem, vmem],
        out_specs=(vmem, vmem),
        cost_estimate=cost(40_000_000, 300_000),
        compiler_params=params(),
        name="coefficients",
    )(waves, filters)


def spatial_wave(square, screen):
    return jnp.sqrt((two_pi * two_pi) * square + screen * screen)


def source_kernel(screening, parts, source, payload):
    total = parts[0].astype(jnp.float32)
    for at in range(1, CHUNKS):
        total = total + parts[at].astype(jnp.float32)
    total = total * float(ATOMS * XY_DEVICES) ** -0.5
    source[...] = total
    square = wave_square(lax.axis_index("core"), lax.axis_index(SWAP))
    decay = [
        jnp.exp(-plane_gap * spatial_wave(square, screening[plane])) for plane in range(PLANES)
    ]
    planes = [total[:, plane * CHAN : (plane + 1) * CHAN] for plane in range(PLANES)]
    upward = planes[0]
    for plane in range(1, PLANES):
        upward = decay[plane] * upward + planes[plane]
    downward = planes[PLANES - 1]
    for plane in reversed(range(PLANES - 1)):
        downward = decay[plane] * downward + planes[plane]
    layer = lax.axis_index(VERTICAL)
    which = lax.broadcasted_iota(jnp.int32, (8, CHAN), 0)
    screens = jnp.zeros((8, CHAN), jnp.float32)
    for plane in range(PLANES):
        screens = jnp.where(which == plane, screening[plane], screens)
    for target in range(LAYERS):
        payload[target, 0:CHUNK, :] = jnp.where(layer < target, upward, downward)
        payload[target, CHUNK:PAYLOAD, :] = screens


def local_source(screening, parts):
    return pl.pallas_call(
        source_kernel,
        out_shape=(
            jax.ShapeDtypeStruct((CHUNK, COLS), jnp.float32),
            jax.ShapeDtypeStruct((LAYERS, PAYLOAD, CHAN), jnp.float32),
        ),
        in_specs=[smem, vmem],
        out_specs=(vmem, vmem),
        cost_estimate=cost(1_000_000, 600_000),
        compiler_params=params(),
        name="local_source",
    )(screening, parts)


def potential_kernel(screening, source, carried, alpha, beta, out):
    square = wave_square(lax.axis_index("core"), lax.axis_index(SWAP))
    layer = lax.axis_index(VERTICAL)
    upward = jnp.zeros((CHUNK, CHAN), jnp.float32)
    downward = jnp.zeros((CHUNK, CHAN), jnp.float32)
    scales = []
    for at in range(LAYERS):
        depth = jnp.zeros((CHUNK, CHAN), jnp.float32)
        for plane in range(PLANES):
            depth = depth + spatial_wave(square, carried[at, CHUNK + plane : CHUNK + plane + 1, :])
        scales.append(jnp.exp(-plane_gap * depth))
    for at in range(LAYERS):
        upward = jnp.where(at < layer, scales[at] * upward + carried[at, 0:CHUNK, :], upward)
    for at in reversed(range(LAYERS)):
        downward = jnp.where(at > layer, scales[at] * downward + carried[at, 0:CHUNK, :], downward)
    spatial = [spatial_wave(square, screening[plane]) for plane in range(PLANES)]
    decay = [jnp.exp(-plane_gap * s) for s in spatial]
    planes = [source[:, plane * CHAN : (plane + 1) * CHAN] for plane in range(PLANES)]
    sums = []
    for plane in range(PLANES):
        upward = decay[plane] * upward + planes[plane]
        sums.append(upward - planes[plane])
    for plane in reversed(range(PLANES)):
        downward = decay[plane] * downward + planes[plane]
        sums[plane] = sums[plane] + downward
    odd = (lax.broadcasted_iota(jnp.int32, (CHUNK, CHAN), 0) & 1) == 1
    results = []
    for plane in range(PLANES):
        field = sums[plane]
        partner = jnp.where(odd, pltpu.roll(field, 1, 0), pltpu.roll(field, CHUNK - 1, 0))
        mixed = alpha[...] * field + beta[...] * partner
        results.append((long_gain * two_pi) / spatial[plane] * mixed)
    full = jnp.concatenate(results, axis=1).astype(jnp.bfloat16)
    for at in range(CHUNKS):
        out[at] = full


def local_potential(screening, source, carried, alpha, beta):
    return pl.pallas_call(
        potential_kernel,
        out_shape=jax.ShapeDtypeStruct((CHUNKS, CHUNK, COLS), jnp.bfloat16),
        in_specs=[smem, vmem, vmem, vmem, vmem],
        out_specs=vmem,
        cost_estimate=cost(1_000_000, 1_000_000),
        compiler_params=params(),
        name="local_potential",
    )(screening, source, carried, alpha, beta)


def ghost_kernel(rows, features, sent, own, arrived):
    load = pltpu.make_async_copy(features, own, arrived)
    load.start()
    load.wait()

    def eight(at, _):
        for k in range(8):
            sent[at * 8 + k] = own[rows[at * 8 + k]]
        return 0

    lax.fori_loop(0, GHOST // 8, eight, 0)


def ghost_rows(rows, features):
    return pl.pallas_call(
        ghost_kernel,
        out_shape=jax.ShapeDtypeStruct((GHOST, 1, CHAN), jnp.float32),
        in_specs=[smem, anywhere],
        out_specs=vmem,
        scratch_shapes=[pltpu.VMEM((ATOMS, 1, CHAN), jnp.float32), pltpu.SemaphoreType.DMA],
        cost_estimate=cost(1_000, 1_000_000),
        compiler_params=params(56),
        name="ghost_rows",
    )(rows, features)


GROUP = 4
STEP = 8


def load_slots(neighbours, weight, slots, factors, arrived, first, count):
    quarter = count // GROUP
    copies = [
        pltpu.make_async_copy(
            neighbours.at[k, pl.ds(first + j * quarter, quarter)],
            slots[k * GROUP + j],
            arrived.at[k * GROUP + j],
        )
        for k in range(NBR)
        for j in range(GROUP)
    ]
    copies.append(
        pltpu.make_async_copy(
            weight.at[:, pl.ds(first, count)], factors, arrived.at[NBR * GROUP]
        )
    )
    return copies


def weighted_rows(slots, factors, columns, table, sums, count):
    quarter = count // GROUP
    place = lax.broadcasted_iota(jnp.int32, (8, CHAN), 0)
    masks = [place == s for s in range(8)]
    for j in range(GROUP):
        for half in range(2):
            columns[:, half * GROUP + j, :] = jnp.transpose(
                factors[half * 8 : half * 8 + 8, j * quarter : (j + 1) * quarter]
            )

    def step(at, _):
        for g in range(STEP):
            group = at * STEP + g
            factor = columns[group]
            total = None
            for k in range(8):
                picked = None
                for half in range(2):
                    for j in range(GROUP):
                        row = slots[(k + 8 * half) * GROUP + j][group]
                        found = jnp.broadcast_to(table[row], (8, CHAN))
                        mask = masks[half * GROUP + j]
                        picked = found if picked is None else jnp.where(mask, found, picked)
                term = picked * factor[:, k : k + 1]
                total = term if total is None else total + term
            total = total + pltpu.roll(total, GROUP, 0)
            sums[pl.ds(group, GROUP, stride=quarter), :] = total[0:GROUP]
        return 0

    lax.fori_loop(0, quarter // STEP, step, 0)


def store_messages(sums, projection, short, out, stored, first, count):
    short[...] = jnp.dot(
        sums[...],
        projection[...],
        preferred_element_type=jnp.float32,
        precision=lax.Precision.HIGHEST,
    )
    copy = pltpu.make_async_copy(short, out.at[pl.ds(first, count)], stored)
    copy.start()
    copy.wait()


def pair_scratch(count):
    return [pltpu.SMEM((count // GROUP,), jnp.int32)] * (NBR * GROUP) + [
        pltpu.VMEM((NBR, count), jnp.float32),
        pltpu.VMEM((count // GROUP, 8, 8), jnp.float32),
        pltpu.VMEM((count, CHAN), jnp.float32),
        pltpu.VMEM((count, CHAN), jnp.float32),
        pltpu.SemaphoreType.DMA((NBR * GROUP + 1,)),
        pltpu.SemaphoreType.DMA,
    ]


def first_pairs(neighbours, weight, w_short, features, sides, count):
    def kernel(index, weights, projection, own, a, b, c, d, table, out, *scratch):
        slots = scratch[: NBR * GROUP]
        factors, columns, sums, short, arrived, stored, placed = scratch[NBR * GROUP :]
        loads = load_slots(index, weights, slots, factors, arrived, 0, count)
        core = lax.axis_index("core")
        odd = lax.axis_index(VERTICAL) & 1
        loads.append(pltpu.make_async_copy(own, table.at[pl.ds(0, ATOMS)], placed.at[0]))
        for at, (rows, slot) in enumerate(
            ((a, 1 - core), (b, core), (c, 3 - odd), (d, 2 + odd))
        ):
            start = ATOMS + slot * GHOST
            loads.append(
                pltpu.make_async_copy(rows, table.at[pl.ds(start, GHOST)], placed.at[1 + at])
            )
        for load in loads:
            load.start()
        for load in loads:
            load.wait()
        weighted_rows(slots, factors, columns, table, sums, count)
        store_messages(sums, projection, short, out, stored, 0, count)

    return pl.pallas_call(
        kernel,
        out_shape=(
            jax.ShapeDtypeStruct((TABLE, 1, CHAN), jnp.float32),
            jax.ShapeDtypeStruct((ATOMS, CHAN), jnp.float32),
        ),
        in_specs=[anywhere, anywhere, vmem] + [anywhere] * 5,
        out_specs=(vmem, anywhere),
        scratch_shapes=pair_scratch(count) + [pltpu.SemaphoreType.DMA((5,))],
        cost_estimate=cost(count * 200_000, count * 57_000),
        compiler_params=params(),
        name="first_pairs",
    )(neighbours, weight, w_short, features, *sides)


def more_pairs(neighbours, weight, w_short, table, messages, first, count, name):
    def kernel(index, weights, projection, rows, before, out, *scratch):
        slots = scratch[: NBR * GROUP]
        factors, columns, sums, short, arrived, stored = scratch[NBR * GROUP :]
        loads = load_slots(index, weights, slots, factors, arrived, first, count)
        for load in loads:
            load.start()
        for load in loads:
            load.wait()
        weighted_rows(slots, factors, columns, rows, sums, count)
        store_messages(sums, projection, short, out, stored, first, count)

    return pl.pallas_call(
        kernel,
        out_shape=jax.ShapeDtypeStruct((ATOMS, CHAN), jnp.float32),
        in_specs=[anywhere, anywhere, vmem, vmem, anywhere],
        out_specs=anywhere,
        input_output_aliases={4: 0},
        scratch_shapes=pair_scratch(count),
        cost_estimate=cost(count * 200_000, count * 57_000),
        compiler_params=params(),
        name=name,
    )(neighbours, weight, w_short, table, messages)


def project_kernel(mine, theirs, phase_in, hat, short, out, phase, arrived):
    at = pl.program_id(0)
    loads = [
        pltpu.make_async_copy(phase_in.at[:, pl.ds(i * BLOCK, BLOCK)], phase.at[i], arrived.at[i])
        for i in range(ATOMS // BLOCK)
    ]

    @pl.when(at == 0)
    def _():
        for load in loads:
            load.start()

    for i, load in enumerate(loads):

        @pl.when(at == i)
        def _():
            load.wait()

    atoms = pl.ds(pl.multiple_of(at * BLOCK, BLOCK), BLOCK)
    core = lax.axis_index("core")
    dims = (((0,), (0,)), ((), ()))
    near = pl.multiple_of(core * USED, 16)
    far = pl.multiple_of((1 - core) * USED, 16)
    projected = lax.dot_general(
        mine[0:USED, :], phase[at, pl.ds(near, USED), :], dims, preferred_element_type=jnp.float32
    ) + lax.dot_general(
        theirs[0:USED, :], phase[at, pl.ds(far, USED), :], dims, preferred_element_type=jnp.float32
    )
    total = hat[0:1, atoms] * projected[0:CHAN]
    for plane in range(1, PLANES):
        total = total + hat[plane : plane + 1, atoms] * projected[plane * CHAN : (plane + 1) * CHAN]
    out[...] = jnp.transpose(total) + short[atoms, :]


def project(mine, theirs, phase, hat, short):
    return pl.pallas_call(
        project_kernel,
        grid=(ATOMS // BLOCK,),
        out_shape=jax.ShapeDtypeStruct((ATOMS, CHAN), jnp.float32),
        in_specs=[vmem, vmem, hbm, vmem, vmem],
        out_specs=pl.BlockSpec((BLOCK, CHAN), lambda i: (i, 0)),
        scratch_shapes=[
            pltpu.VMEM((ATOMS // BLOCK, 2 * USED, BLOCK), jnp.bfloat16),
            pltpu.SemaphoreType.DMA((ATOMS // BLOCK,)),
        ],
        cost_estimate=cost(1_500_000_000, 6_000_000),
        compiler_params=params(50),
        name="project",
    )(mine, theirs, phase, hat, short)


PIECES = (512, 512, 1024)


def swapped(value, axis, start):
    count = lax.axis_size(axis)
    ring = axis == LATERAL
    route = []
    for low in range(start, count, 2):
        if low + 1 < count or ring:
            high = (low + 1) % count
            route += [(low, high), (high, low)]
    return lax.ppermute(value, axis, route)


def other_core(value):
    return lax.ppermute(value, "core", [(0, 1), (1, 0)])


def on_device(
    features,
    positions,
    plane_index,
    plane_frac,
    neighbours,
    pair_weight,
    ghost_index,
    wave_index,
    channel_filter,
    screening,
    w_short,
):
    tie = lax.optimization_barrier
    own_rows = features.reshape(ATOMS, 1, CHAN)
    sent = ghost_rows(ghost_index, own_rows)
    sent, positions = tie((sent, positions))
    sides = [
        swapped(sent, LATERAL, 0),
        swapped(sent, LATERAL, 1),
        swapped(sent, VERTICAL, 0),
        swapped(sent, VERTICAL, 1),
    ]
    phase, hat, own, other = local_structure(
        positions, plane_index.reshape(1, -1), plane_frac.reshape(1, -1), features
    )
    own, other, *_ = tie((own, other, *sides))
    joined = (own + other_core(other).astype(jnp.float32)).astype(jnp.bfloat16)
    joined = joined.reshape(CHUNKS, CHUNK, COLS)
    joined, waves, slots, weights = tie((joined, wave_index, neighbours, pair_weight))
    parts = lax.all_to_all(joined, SWAP, 0, 0)
    alpha, beta = coefficients(waves, channel_filter)
    first, second = PIECES[0], PIECES[0] + PIECES[1]
    table, short = first_pairs(slots, weights, w_short, own_rows, sides, first)

    parts, short, alpha, beta = tie((parts, short, alpha, beta))
    source, payload = local_source(screening, parts)
    payload, short = tie((payload, short))
    carried = lax.all_to_all(payload, VERTICAL, 0, 0)
    short = more_pairs(
        slots, weights, w_short, table, short, first, PIECES[1], "second_pairs"
    )

    carried, short = tie((carried, short))
    field = local_potential(screening, source, carried, alpha, beta)
    field, short = tie((field, short))
    mine = lax.all_to_all(field, SWAP, 0, 0)
    short = more_pairs(
        slots, weights, w_short, table, short, second, PIECES[2], "third_pairs"
    )

    mine, short = tie((mine, short))
    mine = mine.reshape(HALF, COLS)
    theirs = other_core(mine)
    return project(mine, theirs, phase, hat, short)


def solution(mesh):
    split = Mesh(mesh.devices.reshape(8, 2, 2, 2, 4), SPLIT)
    return jax.shard_map(
        on_device,
        mesh=split,
        in_specs=(
            P(SPLIT, None),
            P(None, SPLIT),
            P(SPLIT),
            P(SPLIT),
            P(None, SPLIT),
            P(None, SPLIT),
            P(SPLIT),
            P(),
            P(),
            P(VERTICAL),
            P(),
        ),
        out_specs=P(SPLIT, None),
        check_vma=False,
    )
```

```python
import math

import jax
import jax.numpy as jnp
from jax import lax
from jax.experimental import pallas as pl
from jax.experimental.pallas import tpu as pltpu
from jax.sharding import Mesh
from jax.sharding import PartitionSpec as P

two_pi = 2.0 * math.pi
plane_gap = 0.01
long_gain = 0.125

ATOMS = 2048
CHAN = 128
PLANES = 4
COLS = PLANES * CHAN
NBR = 16
GHOST = 256
TABLE = ATOMS + 4 * GHOST
LAYERS = 8
XY_DEVICES = 32
CHUNK = 24
CHUNKS = 16
HALF = CHUNKS * CHUNK
USED = 14 * CHUNK
PAYLOAD = 32

SPLIT = ("z", "xl", "core", "xh", "y")
LATERAL = ("z", "xl", "core")
SWAP = ("z", "xl")
VERTICAL = ("xh", "y")

smem = pl.BlockSpec(memory_space=pltpu.SMEM)
vmem = pl.BlockSpec(memory_space=pltpu.VMEM)
anywhere = pl.BlockSpec(memory_space=pl.ANY)
hbm = pl.BlockSpec(memory_space=pltpu.HBM)


def cost(flops, nbytes):
    return pl.CostEstimate(flops=flops, bytes_accessed=nbytes, transcendentals=0)


def params(mebibytes=8):
    return pltpu.CompilerParams(vmem_limit_bytes=mebibytes << 20)


BLOCK = 512


def structure_kernel(
    positions,
    plane_low,
    plane_height,
    features,
    phase_out,
    hat,
    own,
    other,
    phase,
    weighted,
    pos,
    low,
    frac,
    feat,
    arrived,
    kept,
):
    loads = [
        pltpu.make_async_copy(source, target, arrived.at[at])
        for at, (source, target) in enumerate(
            ((positions, pos), (plane_low, low), (plane_height, frac), (features, feat))
        )
    ]
    for load in loads:
        load.start()
    for load in loads:
        load.wait()
    keep = pltpu.make_async_copy(phase, phase_out, kept)
    tile_row = lax.broadcasted_iota(jnp.int32, (8, BLOCK), 0)
    upper = tile_row >= 4
    role = tile_row & 3
    wave_is_sin_x = (role == 1) | (role == 2)
    wave_is_sin_y = (role & 1) == 1
    orders = lax.broadcasted_iota(jnp.int32, (16, BLOCK), 0).astype(jnp.float32)

    def row(table, at):
        return jnp.broadcast_to(table[at : at + 1, :], (8, BLOCK))

    def block(at, _):
        lanes = pl.ds(pl.multiple_of(at * BLOCK, BLOCK), BLOCK)

        def tables(coordinate):
            turns = orders * coordinate
            turns = turns - jnp.floor(turns + 0.5)
            angle = two_pi * turns
            return jnp.cos(angle), jnp.sin(angle)

        cos_x, sin_x = tables(pos[0:1, lanes])
        cos_y, sin_y = tables(pos[1:2, lanes])
        for half in range(2):
            b_tiles, axis_tiles = [], []
            for tile in range(3):
                n = 6 * half + 1 + 2 * tile
                cos_n = jnp.where(upper, row(cos_y, n + 1), row(cos_y, n))
                sin_n = jnp.where(upper, row(sin_y, n + 1), row(sin_y, n))
                b_tiles.append(jnp.where(wave_is_sin_y, sin_n, cos_n))
                cos_m = jnp.where(upper, row(cos_x, n + 1), row(cos_x, n))
                sin_m = jnp.where(upper, row(sin_x, n + 1), row(sin_x, n))
                axis_tiles.append(
                    jnp.where(
                        role == 0,
                        cos_n,
                        jnp.where(role == 1, cos_m, jnp.where(role == 2, sin_m, sin_n)),
                    )
                )
            for pair in range(6):
                parts = []
                for a in (2 * pair + 1, 2 * pair + 2):
                    a_tile = jnp.where(wave_is_sin_x, row(sin_x, a), row(cos_x, a))
                    parts += [a_tile * b_tile for b_tile in b_tiles]
                rows = half * USED + pair * 2 * CHUNK
                phase[rows : rows + 2 * CHUNK, lanes] = jnp.concatenate(parts, axis=0).astype(
                    jnp.bfloat16
                )
            zero = jnp.zeros((8, BLOCK), jnp.float32)
            first = jnp.where(tile_row == 0, 1.0, 0.0) if half == 0 else zero
            rows = half * USED + 12 * CHUNK
            phase[rows : rows + 2 * CHUNK, lanes] = jnp.concatenate(
                axis_tiles + [first, zero, zero], axis=0
            ).astype(jnp.bfloat16)

        low_plane = low[:, lanes]
        height = frac[:, lanes]
        hat_block = jnp.where(tile_row == low_plane, 1.0 - height, 0.0) + jnp.where(
            tile_row == low_plane + 1, height, 0.0
        )
        hat[:, lanes] = hat_block
        hat_cols = jnp.transpose(hat_block)
        feat_block = feat[lanes, :]
        for plane in range(PLANES):
            weighted[lanes, plane * CHAN : (plane + 1) * CHAN] = (
                hat_cols[:, plane : plane + 1] * feat_block
            ).astype(jnp.bfloat16)
        return 0

    lax.fori_loop(0, ATOMS // BLOCK, block, 0)
    keep.start()
    core = lax.axis_index("core")
    for mine in (False, True):
        start = pl.multiple_of((core if mine else 1 - core) * USED, 16)
        sums = jnp.dot(
            phase[pl.ds(start, USED), :], weighted[...], preferred_element_type=jnp.float32
        )
        rest = jnp.zeros((HALF - USED, COLS), jnp.float32)
        if mine:
            own[0:USED, :] = sums
            own[USED:HALF, :] = rest
        else:
            other[0:USED, :] = sums.astype(jnp.bfloat16)
            other[USED:HALF, :] = rest.astype(jnp.bfloat16)
    keep.wait()


def local_structure(positions, low, frac, features):
    return pl.pallas_call(
        structure_kernel,
        out_shape=(
            jax.ShapeDtypeStruct((2 * USED, ATOMS), jnp.bfloat16),
            jax.ShapeDtypeStruct((8, ATOMS), jnp.float32),
            jax.ShapeDtypeStruct((HALF, COLS), jnp.float32),
            jax.ShapeDtypeStruct((HALF, COLS), jnp.bfloat16),
        ),
        in_specs=[hbm, hbm, hbm, hbm],
        out_specs=(hbm, vmem, vmem, vmem),
        scratch_shapes=[
            pltpu.VMEM((2 * USED, ATOMS), jnp.bfloat16),
            pltpu.VMEM((ATOMS, COLS), jnp.bfloat16),
            pltpu.VMEM((2, ATOMS), jnp.float32),
            pltpu.VMEM((1, ATOMS), jnp.int32),
            pltpu.VMEM((1, ATOMS), jnp.float32),
            pltpu.VMEM((ATOMS, CHAN), jnp.float32),
            pltpu.SemaphoreType.DMA((4,)),
            pltpu.SemaphoreType.DMA,
        ],
        cost_estimate=cost(1_500_000_000, 8_000_000),
        compiler_params=params(60),
        name="local_structure",
    )(positions, low, frac, features)


def wave_square(half, chunk):
    place = lax.broadcasted_iota(jnp.int32, (CHUNK, CHAN), 0)
    n = 6 * half + 1 + (place >> 2)
    n_square = jnp.where(chunk <= 12, n * n, 0)
    a_square = jnp.where(chunk < 12, (chunk + 1) * (chunk + 1), 0)
    return (n_square + a_square).astype(jnp.float32)


def coefficient_kernel(waves, filters, alpha, beta):
    half, chunk = lax.axis_index("core"), lax.axis_index(SWAP)
    place = lax.broadcasted_iota(jnp.int32, (CHUNK, 512), 0)
    role = place & 3
    n = 6 * half + 1 + (place >> 2)
    along_x = (role == 1) | (role == 2)
    only_zero = jnp.where((place == 0) & (chunk == 13) & (half == 0), 0, -1)
    a = jnp.where(chunk < 12, chunk + 1, jnp.where(chunk == 12, jnp.where(along_x, n, 0), only_zero))
    b = jnp.where(chunk < 12, n, jnp.where(chunk == 12, jnp.where(along_x, 0, n), only_zero))
    kx, ky = waves[0:1, :], waves[1:2, :]
    hit = jnp.where((jnp.abs(kx) == a) & (jnp.abs(ky) == b), 1.0, 0.0)
    product = kx * ky
    sign = jnp.where(product > 0, 1.0, jnp.where(product < 0, -1.0, 0.0))
    signed = hit * sign * jnp.where(role < 2, -1.0, 1.0)
    both = jnp.dot(
        jnp.concatenate([hit, signed], axis=0),
        filters[...],
        preferred_element_type=jnp.float32,
        precision=lax.Precision.HIGHEST,
    )
    alpha[...] = both[0:CHUNK]
    beta[...] = both[CHUNK : 2 * CHUNK]


def coefficients(waves, filters):
    return pl.pallas_call(
        coefficient_kernel,
        out_shape=(jax.ShapeDtypeStruct((CHUNK, CHAN), jnp.float32),) * 2,
        in_specs=[vmem, vmem],
        out_specs=(vmem, vmem),
        cost_estimate=cost(40_000_000, 300_000),
        compiler_params=params(),
        name="coefficients",
    )(waves, filters)


def spatial_wave(square, screen):
    return jnp.sqrt((two_pi * two_pi) * square + screen * screen)


def source_kernel(screening, parts, source, payload):
    total = parts[0].astype(jnp.float32)
    for at in range(1, CHUNKS):
        total = total + parts[at].astype(jnp.float32)
    total = total * float(ATOMS * XY_DEVICES) ** -0.5
    source[...] = total
    square = wave_square(lax.axis_index("core"), lax.axis_index(SWAP))
    decay = [
        jnp.exp(-plane_gap * spatial_wave(square, screening[plane])) for plane in range(PLANES)
    ]
    planes = [total[:, plane * CHAN : (plane + 1) * CHAN] for plane in range(PLANES)]
    upward = planes[0]
    for plane in range(1, PLANES):
        upward = decay[plane] * upward + planes[plane]
    downward = planes[PLANES - 1]
    for plane in reversed(range(PLANES - 1)):
        downward = decay[plane] * downward + planes[plane]
    layer = lax.axis_index(VERTICAL)
    which = lax.broadcasted_iota(jnp.int32, (8, CHAN), 0)
    screens = jnp.zeros((8, CHAN), jnp.float32)
    for plane in range(PLANES):
        screens = jnp.where(which == plane, screening[plane], screens)
    for target in range(LAYERS):
        payload[target, 0:CHUNK, :] = jnp.where(layer < target, upward, downward)
        payload[target, CHUNK:PAYLOAD, :] = screens


def local_source(screening, parts):
    return pl.pallas_call(
        source_kernel,
        out_shape=(
            jax.ShapeDtypeStruct((CHUNK, COLS), jnp.float32),
            jax.ShapeDtypeStruct((LAYERS, PAYLOAD, CHAN), jnp.float32),
        ),
        in_specs=[smem, vmem],
        out_specs=(vmem, vmem),
        cost_estimate=cost(1_000_000, 600_000),
        compiler_params=params(),
        name="local_source",
    )(screening, parts)


def potential_kernel(screening, source, carried, alpha, beta, out):
    square = wave_square(lax.axis_index("core"), lax.axis_index(SWAP))
    layer = lax.axis_index(VERTICAL)
    upward = jnp.zeros((CHUNK, CHAN), jnp.float32)
    downward = jnp.zeros((CHUNK, CHAN), jnp.float32)
    scales = []
    for at in range(LAYERS):
        depth = jnp.zeros((CHUNK, CHAN), jnp.float32)
        for plane in range(PLANES):
            depth = depth + spatial_wave(square, carried[at, CHUNK + plane : CHUNK + plane + 1, :])
        scales.append(jnp.exp(-plane_gap * depth))
    for at in range(LAYERS):
        upward = jnp.where(at < layer, scales[at] * upward + carried[at, 0:CHUNK, :], upward)
    for at in reversed(range(LAYERS)):
        downward = jnp.where(at > layer, scales[at] * downward + carried[at, 0:CHUNK, :], downward)
    spatial = [spatial_wave(square, screening[plane]) for plane in range(PLANES)]
    decay = [jnp.exp(-plane_gap * s) for s in spatial]
    planes = [source[:, plane * CHAN : (plane + 1) * CHAN] for plane in range(PLANES)]
    sums = []
    for plane in range(PLANES):
        upward = decay[plane] * upward + planes[plane]
        sums.append(upward - planes[plane])
    for plane in reversed(range(PLANES)):
        downward = decay[plane] * downward + planes[plane]
        sums[plane] = sums[plane] + downward
    odd = (lax.broadcasted_iota(jnp.int32, (CHUNK, CHAN), 0) & 1) == 1
    results = []
    for plane in range(PLANES):
        field = sums[plane]
        partner = jnp.where(odd, pltpu.roll(field, 1, 0), pltpu.roll(field, CHUNK - 1, 0))
        mixed = alpha[...] * field + beta[...] * partner
        results.append((long_gain * two_pi) / spatial[plane] * mixed)
    full = jnp.concatenate(results, axis=1).astype(jnp.bfloat16)
    for at in range(CHUNKS):
        out[at] = full


def local_potential(screening, source, carried, alpha, beta):
    return pl.pallas_call(
        potential_kernel,
        out_shape=jax.ShapeDtypeStruct((CHUNKS, CHUNK, COLS), jnp.bfloat16),
        in_specs=[smem, vmem, vmem, vmem, vmem],
        out_specs=vmem,
        cost_estimate=cost(1_000_000, 1_000_000),
        compiler_params=params(),
        name="local_potential",
    )(screening, source, carried, alpha, beta)


def ghost_kernel(rows, features, sent, own, arrived):
    load = pltpu.make_async_copy(features, own, arrived)
    load.start()
    load.wait()

    def eight(at, _):
        for k in range(8):
            sent[at * 8 + k] = own[rows[at * 8 + k]]
        return 0

    lax.fori_loop(0, GHOST // 8, eight, 0)


def ghost_rows(rows, features):
    return pl.pallas_call(
        ghost_kernel,
        out_shape=jax.ShapeDtypeStruct((GHOST, 1, CHAN), jnp.float32),
        in_specs=[smem, anywhere],
        out_specs=vmem,
        scratch_shapes=[pltpu.VMEM((ATOMS, 1, CHAN), jnp.float32), pltpu.SemaphoreType.DMA],
        cost_estimate=cost(1_000, 1_000_000),
        compiler_params=params(56),
        name="ghost_rows",
    )(rows, features)


GROUP = 4
STEP = 8


def load_slots(neighbours, weight, slots, factors, arrived, first, count):
    quarter = count // GROUP
    copies = [
        pltpu.make_async_copy(
            neighbours.at[k, pl.ds(first + j * quarter, quarter)],
            slots[k * GROUP + j],
            arrived.at[k * GROUP + j],
        )
        for k in range(NBR)
        for j in range(GROUP)
    ]
    copies.append(
        pltpu.make_async_copy(
            weight.at[:, pl.ds(first, count)], factors, arrived.at[NBR * GROUP]
        )
    )
    return copies


def weighted_rows(slots, factors, columns, table, sums, count):
    quarter = count // GROUP
    place = lax.broadcasted_iota(jnp.int32, (8, CHAN), 0)
    masks = [place == s for s in range(8)]
    for j in range(GROUP):
        for half in range(2):
            columns[:, half * GROUP + j, :] = jnp.transpose(
                factors[half * 8 : half * 8 + 8, j * quarter : (j + 1) * quarter]
            )

    def step(at, _):
        for g in range(STEP):
            group = at * STEP + g
            factor = columns[group]
            total = None
            for k in range(8):
                picked = None
                for half in range(2):
                    for j in range(GROUP):
                        row = slots[(k + 8 * half) * GROUP + j][group]
                        found = jnp.broadcast_to(table[row], (8, CHAN))
                        mask = masks[half * GROUP + j]
                        picked = found if picked is None else jnp.where(mask, found, picked)
                term = picked * factor[:, k : k + 1]
                total = term if total is None else total + term
            total = total + pltpu.roll(total, GROUP, 0)
            sums[pl.ds(group, GROUP, stride=quarter), :] = total[0:GROUP]
        return 0

    lax.fori_loop(0, quarter // STEP, step, 0)


def store_messages(sums, projection, short, out, stored, first, count):
    short[...] = jnp.dot(
        sums[...],
        projection[...],
        preferred_element_type=jnp.float32,
        precision=lax.Precision.HIGHEST,
    )
    copy = pltpu.make_async_copy(short, out.at[pl.ds(first, count)], stored)
    copy.start()
    copy.wait()


def pair_scratch(count):
    return [pltpu.SMEM((count // GROUP,), jnp.int32)] * (NBR * GROUP) + [
        pltpu.VMEM((NBR, count), jnp.float32),
        pltpu.VMEM((count // GROUP, 8, 8), jnp.float32),
        pltpu.VMEM((count, CHAN), jnp.float32),
        pltpu.VMEM((count, CHAN), jnp.float32),
        pltpu.SemaphoreType.DMA((NBR * GROUP + 1,)),
        pltpu.SemaphoreType.DMA,
    ]


def table_kernel(own, a, b, c, d, table, placed):
    core = lax.axis_index("core")
    odd = lax.axis_index(VERTICAL) & 1
    copies = [pltpu.make_async_copy(own, table.at[pl.ds(0, ATOMS)], placed.at[0])]
    for at, (rows, slot) in enumerate(((a, 1 - core), (b, core), (c, 3 - odd), (d, 2 + odd))):
        start = ATOMS + slot * GHOST
        copies.append(pltpu.make_async_copy(rows, table.at[pl.ds(start, GHOST)], placed.at[1 + at]))
    for copy in copies:
        copy.start()
    for copy in copies:
        copy.wait()


def lookup_table(features, sides):
    return pl.pallas_call(
        table_kernel,
        out_shape=jax.ShapeDtypeStruct((TABLE, 1, CHAN), jnp.float32),
        in_specs=[anywhere] * 5,
        out_specs=vmem,
        scratch_shapes=[pltpu.SemaphoreType.DMA((5,))],
        cost_estimate=cost(1_000, 3_000_000),
        compiler_params=params(),
        name="lookup_table",
    )(features, *sides)


def pair_messages(neighbours, weight, w_short, table, messages, first, count, name):
    def kernel(index, weights, projection, rows, *rest):
        out, *scratch = rest if messages is None else rest[1:]
        slots = scratch[: NBR * GROUP]
        factors, columns, sums, short, arrived, stored = scratch[NBR * GROUP :]
        loads = load_slots(index, weights, slots, factors, arrived, first, count)
        for load in loads:
            load.start()
        for load in loads:
            load.wait()
        weighted_rows(slots, factors, columns, rows, sums, count)
        store_messages(sums, projection, short, out, stored, first, count)

    earlier = [] if messages is None else [messages]
    return pl.pallas_call(
        kernel,
        out_shape=jax.ShapeDtypeStruct((ATOMS, CHAN), jnp.float32),
        in_specs=[anywhere, anywhere, vmem, vmem] + [anywhere] * len(earlier),
        out_specs=anywhere,
        input_output_aliases={4: 0} if earlier else {},
        scratch_shapes=pair_scratch(count),
        cost_estimate=cost(count * 200_000, count * 57_000),
        compiler_params=params(),
        name=name,
    )(neighbours, weight, w_short, table, *earlier)


def project_kernel(mine, theirs, phase_in, hat, short, out, phase, arrived):
    at = pl.program_id(0)
    loads = [
        pltpu.make_async_copy(phase_in.at[:, pl.ds(i * BLOCK, BLOCK)], phase.at[i], arrived.at[i])
        for i in range(ATOMS // BLOCK)
    ]

    @pl.when(at == 0)
    def _():
        for load in loads:
            load.start()

    for i, load in enumerate(loads):

        @pl.when(at == i)
        def _():
            load.wait()

    atoms = pl.ds(pl.multiple_of(at * BLOCK, BLOCK), BLOCK)
    core = lax.axis_index("core")
    dims = (((0,), (0,)), ((), ()))
    near = pl.multiple_of(core * USED, 16)
    far = pl.multiple_of((1 - core) * USED, 16)
    projected = lax.dot_general(
        mine[0:USED, :], phase[at, pl.ds(near, USED), :], dims, preferred_element_type=jnp.float32
    ) + lax.dot_general(
        theirs[0:USED, :], phase[at, pl.ds(far, USED), :], dims, preferred_element_type=jnp.float32
    )
    total = hat[0:1, atoms] * projected[0:CHAN]
    for plane in range(1, PLANES):
        total = total + hat[plane : plane + 1, atoms] * projected[plane * CHAN : (plane + 1) * CHAN]
    out[...] = jnp.transpose(total) + short[atoms, :]


def project(mine, theirs, phase, hat, short):
    return pl.pallas_call(
        project_kernel,
        grid=(ATOMS // BLOCK,),
        out_shape=jax.ShapeDtypeStruct((ATOMS, CHAN), jnp.float32),
        in_specs=[vmem, vmem, hbm, vmem, vmem],
        out_specs=pl.BlockSpec((BLOCK, CHAN), lambda i: (i, 0)),
        scratch_shapes=[
            pltpu.VMEM((ATOMS // BLOCK, 2 * USED, BLOCK), jnp.bfloat16),
            pltpu.SemaphoreType.DMA((ATOMS // BLOCK,)),
        ],
        cost_estimate=cost(1_500_000_000, 6_000_000),
        compiler_params=params(50),
        name="project",
    )(mine, theirs, phase, hat, short)


PIECES = (512, 512, 1024)


def swapped(value, axis, start):
    count = lax.axis_size(axis)
    ring = axis == LATERAL
    route = []
    for low in range(start, count, 2):
        if low + 1 < count or ring:
            high = (low + 1) % count
            route += [(low, high), (high, low)]
    return lax.ppermute(value, axis, route)


def other_core(value):
    return lax.ppermute(value, "core", [(0, 1), (1, 0)])


def on_device(
    features,
    positions,
    plane_index,
    plane_frac,
    neighbours,
    pair_weight,
    ghost_index,
    wave_index,
    channel_filter,
    screening,
    w_short,
):
    tie = lax.optimization_barrier
    own_rows = features.reshape(ATOMS, 1, CHAN)
    sent = ghost_rows(ghost_index, own_rows)
    sent, positions = tie((sent, positions))
    sides = [
        swapped(sent, LATERAL, 0),
        swapped(sent, LATERAL, 1),
        swapped(sent, VERTICAL, 0),
        swapped(sent, VERTICAL, 1),
    ]
    phase, hat, own, other = local_structure(
        positions, plane_index.reshape(1, -1), plane_frac.reshape(1, -1), features
    )
    own, other, *sides = tie((own, other, *sides))
    table = lookup_table(own_rows, sides)
    own, other, table = tie((own, other, table))
    joined = (own + other_core(other).astype(jnp.float32)).astype(jnp.bfloat16)
    joined = joined.reshape(CHUNKS, CHUNK, COLS)
    joined, waves, slots, weights = tie((joined, wave_index, neighbours, pair_weight))
    parts = lax.all_to_all(joined, SWAP, 0, 0)
    alpha, beta = coefficients(waves, channel_filter)
    first, second = PIECES[0], PIECES[0] + PIECES[1]
    short = pair_messages(slots, weights, w_short, table, None, 0, first, "first_pairs")

    parts, short, alpha, beta = tie((parts, short, alpha, beta))
    source, payload = local_source(screening, parts)
    payload, short = tie((payload, short))
    carried = lax.all_to_all(payload, VERTICAL, 0, 0)
    short = pair_messages(
        slots, weights, w_short, table, short, first, PIECES[1], "second_pairs"
    )

    carried, short = tie((carried, short))
    field = local_potential(screening, source, carried, alpha, beta)
    field, short = tie((field, short))
    mine = lax.all_to_all(field, SWAP, 0, 0)
    short = pair_messages(
        slots, weights, w_short, table, short, second, PIECES[2], "third_pairs"
    )

    mine, short = tie((mine, short))
    mine = mine.reshape(HALF, COLS)
    theirs = other_core(mine)
    return project(mine, theirs, phase, hat, short)


def solution(mesh):
    split = Mesh(mesh.devices.reshape(8, 2, 2, 2, 4), SPLIT)
    return jax.shard_map(
        on_device,
        mesh=split,
        in_specs=(
            P(SPLIT, None),
            P(None, SPLIT),
            P(SPLIT),
            P(SPLIT),
            P(None, SPLIT),
            P(None, SPLIT),
            P(SPLIT),
            P(),
            P(),
            P(VERTICAL),
            P(),
        ),
        out_specs=P(SPLIT, None),
        check_vma=False,
    )
```
